128 devices in a mesh: kvh: 8 (over y, core), split: 16 (over z, x).
Axes of the slice: x: 4, y: 4, z: 4, core: 2. Of those that a mesh axis runs over, the one named last changes fastest.
Arguments:
- queries: bfloat16 [8, 64, 64, 128], P('kvh', 'split'), may hold values from -600 to 600, as said below
- tree_keys: bfloat16 [8, 64, 8, 128], P('kvh', 'split'), may hold values from -16 to 16
- tree_values: bfloat16 [8, 64, 8, 128], P('kvh', 'split'), may hold values from -6 to 6
- key_cache: bfloat16 [8, 3072, 128, 128], P('kvh', 'split'), may hold values from -6 to 6
- value_cache: bfloat16 [8, 3072, 128, 128], P('kvh', 'split'), may hold values from -6 to 6
- page_request: int32 [3072], P('split'), may hold values from 0 to 7, as said below
- page_index: int32 [3072], P('split'), may hold values from 0 to 383, as said below
- ctx_len: int32 [8], replicated, may hold values from 24576 to 49152, as said below
- tree_len: int32 [8], replicated, may hold values from 16 to 64, as said below
- tree_mask: int32 [8, 64, 64], replicated, may hold values from 0 to 1, as said below
Outputs:
- attended: bfloat16 [8, 64, 64, 128], P('kvh', 'split')
The draws below stay inside these ranges and needn't reach their ends.
Inputs may be any that keep to these rules, and one draw needn't show every extreme that they name: `page_request`: each request owns exactly 384 physical pages, spread over the devices in an order drawn from the seed. `page_index`: within one request every place 0 to 383 appears once. `ctx_len`: some request has exactly 49152 cached tokens. `tree_len`: some request has exactly 64 draft tokens. `tree_mask`: row i holds 1 at i and at the ancestors of draft token i in its tree, whose parents come earlier; 0 elsewhere. `queries`: query entries.
All inputs are finite; a program needn't handle non-finite values.
Results may differ from the reference program's by a relative error of at most 0.0085.
Values may be sent and summed in bfloat16 or wider, within the bound.
No kernel may reach another device: no remote copies, remote signals or barrier semaphores. Data moves between devices by JAX's collectives and lax.ppermute only.
A program may use at most 128 MiB of HBM per device.

```python
import math
import jax
import jax.numpy as jnp
from jax import lax

HD = 128
QPG = 8
KVH = 8
HQ = 64
R = 8
TREE = 64
PAGE = 128
BLK = 8
NPAGES = 3072
MAXPAGES = 384
MAXLEN = 49152


def placement_table(key):
    order = jax.random.permutation(jax.random.fold_in(key, 101), NPAGES).astype(jnp.int32)
    logical = jnp.arange(NPAGES, dtype=jnp.int32)
    owner = jnp.zeros((NPAGES,), jnp.int32).at[order].set(logical // MAXPAGES)
    place = jnp.zeros((NPAGES,), jnp.int32).at[order].set(logical % MAXPAGES)
    return (owner, place)


def query_base(key):
    inner = jax.random.fold_in(key, 7)
    return jax.random.truncated_normal(jax.random.fold_in(inner, 1), -6.0, 6.0, (R, TREE, HQ, HD), jnp.float32)


def draw_page_request(key, part):
    owner, place = placement_table(key)
    return owner


def draw_page_index(key, part):
    owner, place = placement_table(key)
    return place


def draw_ctx_len(key, part):
    key = jax.random.fold_in(key, 3)
    value_rows = jax.random.randint(jax.random.fold_in(key, 1), (R,), MAXLEN // 2, MAXLEN + 1).astype(jnp.int32)
    chosen = jax.random.randint(jax.random.fold_in(key, 2), (), 0, R).astype(jnp.int32)
    return jnp.where(jnp.arange(R, dtype=jnp.int32) == chosen, MAXLEN, value_rows).astype(jnp.int32)


def draw_tree_len(key, part):
    key = jax.random.fold_in(key, 5)
    value_rows = jax.random.randint(jax.random.fold_in(key, 1), (R,), TREE // 4, TREE + 1).astype(jnp.int32)
    chosen = jax.random.randint(jax.random.fold_in(key, 2), (), 0, R).astype(jnp.int32)
    return jnp.where(jnp.arange(R, dtype=jnp.int32) == chosen, TREE, value_rows).astype(jnp.int32)


def draw_tree_mask(key, part):
    key = jax.random.fold_in(key, 9)
    raw = jax.random.randint(key, (R, TREE), 0, 1 << 20).astype(jnp.int32)
    slots = jnp.arange(TREE, dtype=jnp.int32)
    parent = raw % jnp.maximum(slots, 1)[None, :]
    parent = jnp.where(slots[None, :] == 0, 0, parent).astype(jnp.int32)
    start = (slots[:, None] == slots[None, :])[None, :, :]
    start = jnp.broadcast_to(start, (R, TREE, TREE))

    def climb(step, state):
        node, anc = state
        node = jnp.take_along_axis(parent, node, axis=1)
        anc = anc | (node[:, :, None] == slots[None, None, :])
        return (node, anc)
    node0 = jnp.broadcast_to(slots[None, :], (R, TREE)).astype(jnp.int32)
    node, anc = lax.fori_loop(0, TREE, climb, (node0, start))
    return anc.astype(jnp.int32)


def draw_queries(key, part):
    base = query_base(key)
    return base.astype(jnp.bfloat16)


def draw_tree_keys(key, part):
    base = query_base(key)
    key = jax.random.fold_in(key, 11)
    target = 1.0 + 0.5 * math.log(MAXLEN)
    coupling = target * QPG / math.sqrt(HD)
    centre = base.reshape(R, TREE, KVH, QPG, HD).mean(axis=3)
    noise = jax.random.normal(jax.random.fold_in(key, 1), (R, TREE, KVH, HD), jnp.float32)
    mixed = coupling * centre + 0.5 * coupling / math.sqrt(QPG) * noise
    return jnp.clip(mixed, -16.0, 16.0).astype(jnp.bfloat16)


def shard_levels(key, extent, cuts, least, top_value):
    factor_of = 1.0
    for axis_at, blocks in cuts:
        steps = jax.random.uniform(jax.random.fold_in(jax.random.fold_in(key, 6), axis_at), (blocks,), jnp.float32, least / len(cuts), top_value / len(cuts))
        factor_of = factor_of * jnp.repeat(jnp.exp(steps), extent[axis_at] // blocks).reshape((-1,) + (1,) * (len(extent) - 1 - axis_at))
    return factor_of


def gaussian(stream_key, dims, scale, bound, shards=(), kind=jnp.bfloat16):
    array = jax.random.normal(stream_key, dims, jnp.float32) * scale
    if len(shards) > 0:
        array = shard_levels(stream_key, dims, shards, -0.22, 0.18) * array
    return jnp.clip(array, min=-bound, max=bound).astype(kind)


def setup_inputs(seed: int = 0) -> dict:
    keys = jax.random.split(jax.random.key(seed), 11)
    return {
        "queries": draw_queries(jax.random.fold_in(keys[10], 71), 0),
        "tree_keys": draw_tree_keys(jax.random.fold_in(keys[10], 71), 0),
        "tree_values": gaussian(keys[2], (R, TREE, KVH, HD), 1.0, 6.0, ((0, 8), (1, 16))),
        "key_cache": gaussian(keys[3], (KVH, NPAGES, PAGE, HD), 1.0, 6.0, ((0, 8), (1, 16))),
        "value_cache": gaussian(keys[4], (KVH, NPAGES, PAGE, HD), 1.0, 6.0, ((0, 8), (1, 16))),
        "page_request": draw_page_request(jax.random.fold_in(keys[10], 71), 0),
        "page_index": draw_page_index(jax.random.fold_in(keys[10], 71), 0),
        "ctx_len": draw_ctx_len(jax.random.fold_in(keys[10], 71), 0),
        "tree_len": draw_tree_len(jax.random.fold_in(keys[10], 71), 0),
        "tree_mask": draw_tree_mask(jax.random.fold_in(keys[10], 71), 0),
    }


def cache_block(carry, item, q_rows, ctx_len):
    run_max, run_sum, running_output = carry
    key_rows, value_rows, owner, index = item
    page = key_rows.shape[1]
    score_scale = key_rows.shape[2] ** -0.5
    selected_rows = jnp.take(q_rows, owner, axis=0).astype(jnp.float32)
    logit_scores = jnp.einsum("zal,zel->zae", selected_rows, key_rows.astype(jnp.float32), precision=lax.Precision.HIGHEST) * score_scale
    limit = jnp.take(ctx_len, owner)
    position = index[:, None] * page + jnp.arange(page, dtype=jnp.int32)[None, :]
    valid = (position < limit[:, None])[:, None, :]
    masked = jnp.where(valid, logit_scores, -1e30)
    page_max = masked.max(axis=2)
    member = owner[:, None] == jnp.arange(R, dtype=jnp.int32)[None, :]
    block_max = jnp.where(member[:, :, None], page_max[:, None, :], -1e30).max(axis=0)
    new_max = jnp.maximum(run_max, block_max)
    shift = jnp.take(new_max, owner, axis=0)
    prob_weights = jnp.where(valid, jnp.exp(masked - shift[:, :, None]), 0.0).astype(jnp.bfloat16)
    widened_rows = prob_weights.astype(jnp.float32)
    partial_output = jnp.einsum("upl,ulz->upz", widened_rows, value_rows.astype(jnp.float32), precision=lax.Precision.HIGHEST)
    part_sum = widened_rows.sum(axis=2)
    one_hot_select = member.astype(jnp.float32)
    rescale_factor = jnp.exp(run_max - new_max)
    run_sum = run_sum * rescale_factor + jnp.einsum("br,bq->rq", one_hot_select, part_sum, precision=lax.Precision.HIGHEST)
    running_output = running_output * rescale_factor[:, :, None] + jnp.einsum("ht,hcg->tcg", one_hot_select, partial_output, precision=lax.Precision.HIGHEST)
    return (new_max, run_sum, running_output), None


def reference(queries, tree_keys, tree_values, key_cache, value_cache, page_request, page_index, ctx_len, tree_len, tree_mask):
    grouped = queries.reshape(R, TREE, KVH, QPG, HD)
    blocks = NPAGES // BLK
    rows = TREE * QPG

    def one_head(head):
        q_head = lax.dynamic_index_in_dim(grouped, head, 2, keepdims=False)
        k_head = lax.dynamic_index_in_dim(key_cache, head, 0, keepdims=False)
        v_head = lax.dynamic_index_in_dim(value_cache, head, 0, keepdims=False)
        q_rows = q_head.reshape(R, rows, HD)
        items = (k_head.reshape(blocks, BLK, PAGE, HD), v_head.reshape(blocks, BLK, PAGE, HD),
                 page_request.reshape(blocks, BLK), page_index.reshape(blocks, BLK))
        start = (jnp.full((R, rows), -1e30, jnp.float32), jnp.zeros((R, rows), jnp.float32),
                 jnp.zeros((R, rows, HD), jnp.float32))
        (cmax, csum, cacc), unused = lax.scan(lambda c, it: cache_block(c, it, q_rows, ctx_len), start, items)
        cmax = cmax.reshape(R, TREE, QPG)
        csum = csum.reshape(R, TREE, QPG)
        cacc = cacc.reshape(R, TREE, QPG, HD)
        tk = lax.dynamic_index_in_dim(tree_keys, head, 2, keepdims=False).astype(jnp.float32)
        tv = lax.dynamic_index_in_dim(tree_values, head, 2, keepdims=False).astype(jnp.float32)
        tscores = jnp.einsum("riqd,rkd->riqk", q_head.astype(jnp.float32), tk, precision=lax.Precision.HIGHEST) * (HD ** -0.5)
        allowed = (tree_mask == 1)[:, :, None, :]
        tmasked = jnp.where(allowed, tscores, -1e30)
        peak = jnp.maximum(cmax, tmasked.max(axis=3))
        tweights = jnp.where(allowed, jnp.exp(tmasked - peak[..., None]), 0.0).astype(jnp.bfloat16).astype(jnp.float32)
        rescale_factor = jnp.exp(cmax - peak)
        total = csum * rescale_factor + tweights.sum(axis=3)
        numer = cacc * rescale_factor[..., None] + jnp.einsum("riqk,rkd->riqd", tweights, tv, precision=lax.Precision.HIGHEST)
        live = (jnp.arange(TREE, dtype=jnp.int32)[None, :] < tree_len[:, None])[:, :, None, None]
        return jnp.where(live, numer / total[..., None], 0.0).astype(jnp.bfloat16)

    outs = lax.map(one_head, jnp.arange(KVH, dtype=jnp.int32))
    return outs.transpose(1, 2, 0, 3, 4).reshape(R, TREE, HQ, HD)
```

```python
import functools

import jax
import jax.numpy as jnp
from jax import lax
from jax.experimental import pallas as pl
from jax.experimental.pallas import tpu as pltpu
from jax.sharding import PartitionSpec as P

BOTH = ("kvh", "split")
NEG = -1e30
LOG2E = 1.4426950408889634
HUGE = 2.0**100
CHUNK = 128
SLOTS = 256
F32 = jnp.float32
BF16 = jnp.bfloat16

NT = (((1,), (1,)), ((), ()))


def column_bias(lims, page):
    col = lax.broadcasted_iota(jnp.int32, (1, page), 1)
    return jnp.concatenate([jnp.where(col < x, 0.0, NEG) for x in lims], 1)


def attn_kernel(
    dims,
    meta,
    x_ref,
    mask_ref,
    k_ref,
    v_ref,
    o_ref,
    m_s,
    l_s,
    acc,
    top,
    plist,
    plim,
    cnt,
):
    requests, splits, tl, group, pages, page, hd = dims
    rows = tl * group
    full_rows = splits * rows
    scale = hd**-0.5 * LOG2E
    i_ctx, i_tl, i_me = 2 * pages, 2 * pages + requests, 2 * pages + 2 * requests

    for r in range(requests):
        cnt[r] = 0

    def scan(p, carry):
        r = meta[p]
        lim = meta[i_ctx + r] - meta[pages + p] * page
        c = cnt[r]
        plist[r * SLOTS + c] = p
        plim[r * SLOTS + c] = lim
        cnt[r] = jnp.where(lim > 0, c + 1, c)
        return carry

    lax.fori_loop(0, pages, scan, 0)

    me = meta[i_me]
    per = splits // requests
    tree_request = me // per
    part = me % per
    tree_rows = full_rows // per
    top[...] = jnp.zeros_like(top)

    def queries(r, count):
        blocks = count // rows
        return x_ref[pl.ds(r * splits, blocks), 0:rows, :].reshape(count, hd)

    def tree_page():
        first = pl.multiple_of(part * tree_rows, tree_rows)
        blk = tree_rows // rows
        q = x_ref[pl.ds(tree_request * splits + part * blk, blk), 0:rows, :]
        kv = x_ref[pl.ds(tree_request * splits, splits), rows : rows + 2 * tl, :]
        kv = kv.reshape(splits * 2 * tl, hd)
        wide = splits * 2 * tl
        values = pltpu.roll(kv.astype(F32), wide - tl, 0).astype(BF16)
        drafts = tree_rows // group
        mask = mask_ref[tree_request, pl.ds(part * drafts, drafts), :]
        tree = mask.shape[1]
        src = lax.broadcasted_iota(jnp.int32, (tree, wide), 0)
        dst = lax.broadcasted_iota(jnp.int32, (tree, wide), 1)
        pick = (src // tl == dst // (2 * tl)) & (src % tl == dst % (2 * tl))
        seen = jnp.dot(
            (mask == 1).astype(F32).astype(BF16),
            pick.astype(F32).astype(BF16),
            preferred_element_type=F32,
        )
        bias = jnp.where(seen > 0.5, 0.0, NEG)
        bias = jnp.broadcast_to(bias[:, None, :], (drafts, group, wide))
        s = lax.dot_general(q.reshape(tree_rows, hd), kv, NT, preferred_element_type=F32)
        return first, s + bias.reshape(tree_rows, wide), values

    def block_of(r, n, start, nb):
        ids, lims = [], []
        for j in range(nb):
            there = start + j < n
            at = r * SLOTS + jnp.minimum(start + j, n)
            ids.append(jnp.where(there, plist[at], 0))
            lims.append(jnp.where(there, plim[at], 0))
        k = jnp.concatenate([k_ref[0, i] for i in ids], 0)
        v = jnp.concatenate([v_ref[0, i] for i in ids], 0)
        return k, v, column_bias(lims, page)

    def add(at, s, v):
        m = m_s[at, :]
        ps = [
            jnp.exp2(s[:, j : j + page] * scale - m) for j in range(0, s.shape[1], page)
        ]
        l_s[at, :] += functools.reduce(jnp.add, ps)
        p = jnp.concatenate([x.astype(BF16) for x in ps], 1)
        acc[at, :] += jnp.dot(p, v, preferred_element_type=F32)

    def add_online(at, s, v):
        old = m_s[at, :]
        new = jnp.maximum(old, jnp.max(s, 1, keepdims=True) * scale)
        m_s[at, :] = new
        fade = jnp.exp2(old - new)
        l_s[at, :] = l_s[at, :] * fade
        acc[at, :] = acc[at, :] * fade
        add(at, s, v)

    def finish(r, count):
        blocks = count // rows
        total = jnp.sum(l_s[0:count, :], 1, keepdims=True)
        total = jnp.broadcast_to(total, (count, hd))
        some = total > 0.0
        safe = jnp.where(some, total, 1.0)
        o = (acc[0:count, :] / safe).astype(BF16)
        o_ref[pl.ds(r * splits, blocks), 0:rows, :] = o.reshape(blocks, rows, hd)
        lse = jnp.where(some, m_s[0:count, :] + jnp.log2(safe), NEG)
        lse = lse.reshape(blocks, tl, group, hd)
        lane = lax.broadcasted_iota(jnp.int32, (1, 1, hd), 2)
        span = hd // tl
        both = lse[:, tl - 1]
        for i in range(tl - 2, -1, -1):
            both = jnp.where(lane < (i + 1) * span, lse[:, i], both)
        high = both.astype(BF16).astype(F32)
        mid = (both - high).astype(BF16).astype(F32)
        low = both - high - mid
        inner = lane % span
        stat = jnp.where(inner == 0, high, jnp.where(inner == 1, mid, low))
        o_ref[pl.ds(r * splits, blocks), rows : rows + group, :] = stat.astype(BF16)
        return total

    def own_scores(r, count):
        for b in range(count // rows):
            for i in range(tl):
                q = x_ref[r * splits + b, i * group : (i + 1) * group, :].astype(F32)
                key = x_ref[r * splits + b, rows + i : rows + i + 1, :].astype(F32)
                s = jnp.sum(q * key, 1, keepdims=True) * scale
                at = b * rows + i * group
                m_s[at : at + group, :] = jnp.broadcast_to(s, (group, hd))

    def request(r, count):
        n = cnt[r]
        at = slice(0, count)
        l_s[...] = jnp.zeros_like(l_s)
        acc[...] = jnp.zeros_like(acc)

        @pl.when(r == tree_request)
        def _():
            own_scores(r, full_rows)
            first, s, v = tree_page()
            add(pl.ds(first, tree_rows), s, v)

        @pl.when(r != tree_request)
        def _():
            own_scores(r, count)

        q = queries(r, count)

        def take(start, nb):
            k, v, bias = block_of(r, n, start, nb)
            s = lax.dot_general(q, k, NT, preferred_element_type=F32)
            add(at, s + bias, v)

        eights = n // 8

        @pl.loop(0, eights)
        def _(b):
            take(b * 8, 8)

        left = (n - eights * 8 + 1) // 2
        start = eights * 8
        for size, when in (
            (8, left == 4),
            (4, (left == 2) | (left == 3)),
        ):

            @pl.when(when)
            def _():
                take(start, size)

        @pl.when((left == 1) | (left == 3))
        def _():
            take(start + jnp.where(left == 3, 4, 0), 2)

        total = finish(r, count)
        high = functools.reduce(
            jnp.maximum, [total[j : j + 8] for j in range(0, count, 8)]
        )
        top[...] = jnp.maximum(top[...], high)

    def request_online(r):
        n = cnt[r]
        at = slice(0, full_rows)
        m_s[...] = jnp.full_like(m_s, NEG)
        l_s[...] = jnp.zeros_like(l_s)
        acc[...] = jnp.zeros_like(acc)

        @pl.when(r == tree_request)
        def _():
            first, s, v = tree_page()
            add_online(pl.ds(first, tree_rows), s, v)

        q = queries(r, full_rows)

        @pl.loop(0, (n + 1) // 2)
        def _(b):
            k, v, bias = block_of(r, n, b * 2, 2)
            s = lax.dot_general(q, k, NT, preferred_element_type=F32)
            add_online(at, s + bias, v)

        finish(r, full_rows)

    @pl.loop(0, requests)
    def _(r):
        chunks = (meta[i_tl + r] * group + CHUNK - 1) // CHUNK
        for c in range(1, full_rows // CHUNK + 1):

            @pl.when(chunks == c)
            def _():
                request(r, c * CHUNK)

    @pl.when(jnp.logical_not(jnp.max(top[...]) < HUGE))
    def _():
        @pl.loop(0, requests)
        def _(r):
            request_online(r)


def attend(meta, x, mask, key_cache, value_cache, dims):
    requests, splits, tl, group, pages, page, hd = dims
    full_rows = splits * tl * group
    smem = pl.BlockSpec(memory_space=pltpu.SMEM)
    vmem = pl.BlockSpec(memory_space=pltpu.VMEM)
    return pl.pallas_call(
        functools.partial(attn_kernel, dims),
        out_shape=jax.ShapeDtypeStruct(x.shape, BF16),
        in_specs=[smem, vmem, vmem, vmem, vmem],
        out_specs=vmem,
        scratch_shapes=[
            pltpu.VMEM((full_rows, hd), F32),
            pltpu.VMEM((full_rows, hd), F32),
            pltpu.VMEM((full_rows, hd), F32),
            pltpu.VMEM((8, hd), F32),
            pltpu.SMEM((requests * SLOTS,), jnp.int32),
            pltpu.SMEM((requests * SLOTS,), jnp.int32),
            pltpu.SMEM((requests,), jnp.int32),
        ],
        compiler_params=pltpu.CompilerParams(vmem_limit_bytes=40 * 2**20),
        name="attend",
    )(meta, x, mask, key_cache, value_cache)


def join_kernel(dims, where_ref, y_ref, o_ref):
    heads, splits, tl, group, hd = dims
    rows = tl * group
    span = hd // tl
    src = lax.broadcasted_iota(jnp.int32, (hd, tl * hd), 0)
    dst = lax.broadcasted_iota(jnp.int32, (hd, tl * hd), 1)
    pick = (src // span == dst // hd) & (src % span < 3)
    pick = pick.astype(F32).astype(BF16)
    first = where_ref[0]
    length = where_ref[1]
    for h in range(heads):
        stat = y_ref[h * splits : (h + 1) * splits, rows : rows + group, :]
        lse = jnp.dot(
            stat.reshape(splits * group, hd), pick, preferred_element_type=F32
        )
        for i in range(tl):
            one = lse[:, i * hd : (i + 1) * hd].reshape(splits, group, hd)
            high = jnp.max(one, 0, keepdims=True)
            w = jnp.exp2(one - high)
            o = y_ref[
                h * splits : (h + 1) * splits, i * group : (i + 1) * group, :
            ].astype(F32)
            res = jnp.sum(w * o, 0) / jnp.sum(w, 0)
            res = jnp.where(first + i < length, res, 0.0)
            o_ref[0, i, h * group : (h + 1) * group, :] = res.astype(BF16)


def join(where, y, dims):
    heads, splits, tl, group, hd = dims
    return pl.pallas_call(
        functools.partial(join_kernel, dims),
        out_shape=jax.ShapeDtypeStruct((1, tl, heads * group, hd), BF16),
        in_specs=[
            pl.BlockSpec(memory_space=pltpu.SMEM),
            pl.BlockSpec(memory_space=pltpu.VMEM),
        ],
        out_specs=pl.BlockSpec(memory_space=pltpu.VMEM),
        name="join",
    )(where, y)


def per_device(
    queries,
    tree_keys,
    tree_values,
    key_cache,
    value_cache,
    page_request,
    page_index,
    ctx_len,
    tree_len,
    tree_mask,
):
    heads = lax.axis_size("kvh")
    splits = lax.axis_size("split")
    unused, tl, hq, hd = queries.shape
    group = hq // heads
    requests = ctx_len.shape[0]
    unused, pages, page, unused = key_cache.shape
    me = lax.axis_index("split").astype(jnp.int32)

    q = queries.reshape(tl, heads, group, hd).transpose(1, 0, 2, 3)
    x = jnp.concatenate(
        [
            q.reshape(heads, tl * group, hd),
            tree_keys[0].transpose(1, 0, 2),
            tree_values[0].transpose(1, 0, 2),
        ],
        1,
    )
    block = x.shape[1]
    x = jnp.broadcast_to(x[:, None], (heads, splits, block, hd))
    x = x.reshape(heads * splits, block, hd)
    x = lax.all_to_all(x, BOTH, 0, 0, tiled=True)

    meta = jnp.concatenate([page_request, page_index, ctx_len, tree_len, me[None]])
    dims = (requests, splits, tl, group, pages, page, hd)
    y = attend(meta, x, tree_mask, key_cache, value_cache, dims)

    y = lax.all_to_all(y, BOTH, 0, 0, tiled=True)
    own = lax.axis_index("kvh")
    where = jnp.stack([me * tl, jnp.take(tree_len, own)])
    return join(where, y, (heads, splits, tl, group, hd))


def solution(mesh):
    shard = P("kvh", "split", None, None)
    return jax.shard_map(
        per_device,
        mesh=mesh,
        in_specs=(shard,) * 5 + (P("split"), P("split"), P(), P(), P()),
        out_specs=shard,
        check_vma=False,
    )
```

```python
import functools

import jax
import jax.numpy as jnp
from jax import lax
from jax.experimental import pallas as pl
from jax.experimental.pallas import tpu as pltpu
from jax.sharding import PartitionSpec as P

BOTH = ("kvh", "split")
NEG = -1e30
LOG2E = 1.4426950408889634
HUGE = 2.0**100
STEP = 16
CHUNK = 64
F32 = jnp.float32
BF16 = jnp.bfloat16

NT = (((1,), (1,)), ((), ()))


def column_bias(lims, page):
    col = lax.broadcasted_iota(jnp.int32, (1, page), 1)
    return jnp.concatenate([jnp.where(col < x, 0.0, NEG) for x in lims], 1)


def prepare_kernel(dims, meta, lists):
    requests, splits, tl, group, pages, page, hd = dims
    i_ctx, i_tl = 2 * pages, 2 * pages + requests
    i_off, i_full, i_edge = pages, pages + requests + 1, pages + 2 * requests + 1
    i_len = pages + 3 * requests + 1
    for r in range(requests):
        lists[i_off + r] = 0
        lists[i_full + r] = 0
        lists[i_edge + r] = 0
        lists[i_len + r] = meta[i_tl + r]
    lists[i_len + requests] = meta[i_tl + requests]

    def tokens(p):
        r = meta[p]
        return r, meta[i_ctx + r] - meta[pages + p] * page

    def count(p, carry):
        r, lim = tokens(p)
        lists[p] = 0
        lists[i_full + r] += jnp.where(lim >= page, 1, 0)
        lists[i_edge + r] += jnp.where((lim > 0) & (lim < page), lim, 0)
        return carry

    lax.fori_loop(0, pages, count, 0)
    total = 0
    for r in range(requests):
        lists[i_off + r] = total
        total += lists[i_full + r] + jnp.where(lists[i_edge + r] > 0, 1, 0)
        lists[i_full + r] = 0
    lists[i_off + requests] = total

    def place(p, carry):
        r, lim = tokens(p)
        n = lists[i_full + r]
        whole = lim >= page

        @pl.when(whole)
        def _():
            lists[lists[i_off + r] + n] = p
            lists[i_full + r] = n + 1

        @pl.when((lim > 0) & (lim < page))
        def _():
            lists[lists[i_off + r + 1] - 1] = p

        return carry

    lax.fori_loop(0, pages, place, 0)


def prepare(meta, dims):
    requests, splits, tl, group, pages, page, hd = dims
    smem = pl.BlockSpec(memory_space=pltpu.SMEM)
    return pl.pallas_call(
        functools.partial(prepare_kernel, dims),
        out_shape=jax.ShapeDtypeStruct((pages + 4 * requests + 2,), jnp.int32),
        in_specs=[smem],
        out_specs=smem,
        compiler_params=pltpu.CompilerParams(vmem_limit_bytes=2**20),
        cost_estimate=pl.CostEstimate(
            flops=0, bytes_accessed=2**24, transcendentals=0
        ),
        name="prepare",
    )(meta)


def attn_kernel(
    dims,
    lists,
    x_ref,
    mask_ref,
    k_hbm,
    v_hbm,
    o_ref,
    k_ref,
    v_ref,
    m_s,
    l_s,
    acc,
    top,
    sems,
):
    requests, splits, tl, group, pages, page, hd = dims
    rows = tl * group
    full_rows = splits * rows
    scale = hd**-0.5 * LOG2E
    i_off, i_full, i_edge = pages, pages + requests + 1, pages + 2 * requests + 1
    i_tl = pages + 3 * requests + 1

    for r in range(requests):

        @pl.loop(lists[i_off + r], lists[i_off + r + 1])
        def _(slot):
            p = lists[slot]
            pltpu.make_async_copy(k_hbm.at[0, p], k_ref.at[slot], sems.at[0, r]).start()
            pltpu.make_async_copy(v_hbm.at[0, p], v_ref.at[slot], sems.at[1, r]).start()

    def arrive(r):
        n = lists[i_off + r + 1] - lists[i_off + r]

        @pl.when(n > 0)
        def _():
            at = pl.ds(0, n)
            for t, (src, dst) in enumerate(((k_hbm, k_ref), (v_hbm, v_ref))):
                pltpu.make_async_copy(src.at[0, at], dst.at[at], sems.at[t, r]).wait()

    me = lists[i_tl + requests]
    per = splits // requests
    tree_request = me // per
    part = me % per
    tree_rows = full_rows // per
    top[...] = jnp.zeros_like(top)

    def queries(r, count):
        blocks = count // rows
        return x_ref[pl.ds(r * splits, blocks), 0:rows, :].reshape(count, hd)

    def tree_page():
        first = pl.multiple_of(part * tree_rows, tree_rows)
        blk = tree_rows // rows
        q = x_ref[pl.ds(tree_request * splits + part * blk, blk), 0:rows, :]
        kv = x_ref[pl.ds(tree_request * splits, splits), rows : rows + 2 * tl, :]
        kv = kv.reshape(splits * 2 * tl, hd)
        wide = splits * 2 * tl
        values = pltpu.roll(kv.astype(F32), wide - tl, 0).astype(BF16)
        drafts = tree_rows // group
        mask = mask_ref[tree_request, pl.ds(part * drafts, drafts), :]
        tree = mask.shape[1]
        src = lax.broadcasted_iota(jnp.int32, (tree, wide), 0)
        dst = lax.broadcasted_iota(jnp.int32, (tree, wide), 1)
        pick = (src // tl == dst // (2 * tl)) & (src % tl == dst % (2 * tl))
        seen = jnp.dot(
            (mask == 1).astype(F32).astype(BF16),
            pick.astype(F32).astype(BF16),
            preferred_element_type=F32,
        )
        bias = jnp.where(seen > 0.5, 0.0, NEG)
        bias = jnp.broadcast_to(bias[:, None, :], (drafts, group, wide))
        s = lax.dot_general(q.reshape(tree_rows, hd), kv, NT, preferred_element_type=F32)
        return first, s + bias.reshape(tree_rows, wide), values

    def whole_block(r, start, nb):
        at = pl.ds(lists[i_off + r] + start, nb)
        return k_ref[at].reshape(nb * page, hd), v_ref[at].reshape(nb * page, hd)

    def last_block(r):
        n = lists[i_full + r]
        left = n % 2
        first = lists[i_off + r]
        edge = lists[i_edge + r]
        one = first + jnp.where(left == 1, n - 1, 0)
        two = first + jnp.where(edge > 0, n, 0)
        bias = column_bias([left * page, edge], page)
        k = jnp.concatenate([k_ref[one], k_ref[two]], 0)
        v = jnp.concatenate([v_ref[one], v_ref[two]], 0)
        return k, v, bias

    def has_last(r):
        return (lists[i_full + r] % 2 == 1) | (lists[i_edge + r] > 0)

    def add(at, where, s, v):
        m = m_s[where, :]
        ps = [
            jnp.exp2(s[:, j : j + page] * scale - m) for j in range(0, s.shape[1], page)
        ]
        l_s[at, :] += functools.reduce(jnp.add, ps)
        p = jnp.concatenate([x.astype(BF16) for x in ps], 1)
        acc[at, :] += jnp.dot(p, v, preferred_element_type=F32)

    def add_online(at, where, s, v):
        old = m_s[where, :]
        new = jnp.maximum(old, jnp.max(s, 1, keepdims=True) * scale)
        m_s[where, :] = new
        fade = jnp.exp2(old - new)
        l_s[at, :] = l_s[at, :] * fade
        acc[at, :] = acc[at, :] * fade
        add(at, where, s, v)

    def finish(r, count):
        blocks = count // rows
        total = jnp.sum(l_s[0:count, :], 1, keepdims=True)
        total = jnp.broadcast_to(total, (count, hd))
        some = total > 0.0
        safe = jnp.where(some, total, 1.0)
        o = (acc[0:count, :] / safe).astype(BF16)
        o_ref[pl.ds(r * splits, blocks), 0:rows, :] = o.reshape(blocks, rows, hd)
        shift = m_s[pl.ds(r * full_rows, count), :]
        lse = jnp.where(some, shift + jnp.log2(safe), NEG)
        lse = lse.reshape(blocks, tl, group, hd)
        lane = lax.broadcasted_iota(jnp.int32, (1, 1, hd), 2)
        span = hd // tl
        both = lse[:, tl - 1]
        for i in range(tl - 2, -1, -1):
            both = jnp.where(lane < (i + 1) * span, lse[:, i], both)
        high = both.astype(BF16).astype(F32)
        mid = (both - high).astype(BF16).astype(F32)
        low = both - high - mid
        inner = lane % span
        stat = jnp.where(inner == 0, high, jnp.where(inner == 1, mid, low))
        o_ref[pl.ds(r * splits, blocks), rows : rows + group, :] = stat.astype(BF16)
        return total

    @pl.loop(0, requests)
    def _(r):
        for b in range(splits):
            for i in range(tl):
                block = r * splits + b
                q = x_ref[block, i * group : (i + 1) * group, :].astype(F32)
                key = x_ref[block, rows + i : rows + i + 1, :].astype(F32)
                s = jnp.sum(q * key, 1, keepdims=True) * scale
                at = pl.multiple_of(block * rows + i * group, group)
                m_s[pl.ds(at, group), :] = jnp.broadcast_to(s, (group, hd))

    def rows_of(r, first, count):
        return pl.ds(pl.multiple_of(r * full_rows + first, 8), count)

    def request(r, count):
        at = slice(0, count)
        where = rows_of(r, 0, count)
        l_s[...] = jnp.zeros_like(l_s)
        acc[...] = jnp.zeros_like(acc)

        @pl.when(r == tree_request)
        def _():
            first, s, v = tree_page()
            add(pl.ds(first, tree_rows), rows_of(r, first, tree_rows), s, v)

        q = queries(r, count)

        def take(start, nb):
            k, v = whole_block(r, start, nb)
            add(at, where, lax.dot_general(q, k, NT, preferred_element_type=F32), v)

        n = lists[i_full + r]
        whole = n // STEP

        @pl.loop(0, whole)
        def _(b):
            take(b * STEP, STEP)

        start = whole * STEP
        size = STEP // 2
        while size > 1:
            there = (n // size) % 2

            @pl.when(there == 1)
            def _(start=start, size=size):
                take(start, size)

            start = start + there * size
            size //= 2

        @pl.when(has_last(r))
        def _():
            k, v, bias = last_block(r)
            s = lax.dot_general(q, k, NT, preferred_element_type=F32)
            add(at, where, s + bias, v)

        total = finish(r, count)
        high = functools.reduce(
            jnp.maximum, [total[j : j + 8] for j in range(0, count, 8)]
        )
        top[...] = jnp.maximum(top[...], high)

    def request_online(r):
        at = slice(0, full_rows)
        where = rows_of(r, 0, full_rows)
        m_s[where, :] = jnp.full((full_rows, hd), NEG, F32)
        l_s[...] = jnp.zeros_like(l_s)
        acc[...] = jnp.zeros_like(acc)

        @pl.when(r == tree_request)
        def _():
            first, s, v = tree_page()
            add_online(pl.ds(first, tree_rows), rows_of(r, first, tree_rows), s, v)

        q = queries(r, full_rows)

        @pl.loop(0, lists[i_full + r] // 2)
        def _(b):
            k, v = whole_block(r, b * 2, 2)
            s = lax.dot_general(q, k, NT, preferred_element_type=F32)
            add_online(at, where, s, v)

        @pl.when(has_last(r))
        def _():
            k, v, bias = last_block(r)
            s = lax.dot_general(q, k, NT, preferred_element_type=F32)
            add_online(at, where, s + bias, v)

        finish(r, full_rows)

    @pl.loop(0, requests)
    def _(r):
        arrive(r)
        chunks = (lists[i_tl + r] * group + CHUNK - 1) // CHUNK
        for c in range(2, full_rows // CHUNK + 1):

            @pl.when((chunks == c) | ((c == 2) & (chunks < 2)))
            def _():
                request(r, c * CHUNK)

    @pl.when(jnp.logical_not(jnp.max(top[...]) < HUGE))
    def _():
        @pl.loop(0, requests)
        def _(r):
            request_online(r)


def attend(lists, x, mask, key_cache, value_cache, dims):
    requests, splits, tl, group, pages, page, hd = dims
    full_rows = splits * tl * group
    smem = pl.BlockSpec(memory_space=pltpu.SMEM)
    vmem = pl.BlockSpec(memory_space=pltpu.VMEM)
    hbm = pl.BlockSpec(memory_space=pltpu.HBM)
    return pl.pallas_call(
        functools.partial(attn_kernel, dims),
        out_shape=jax.ShapeDtypeStruct(x.shape, BF16),
        in_specs=[smem, vmem, vmem, hbm, hbm],
        out_specs=vmem,
        scratch_shapes=[
            pltpu.VMEM((pages, page, hd), BF16),
            pltpu.VMEM((pages, page, hd), BF16),
            pltpu.VMEM((requests * full_rows, hd), F32),
            pltpu.VMEM((full_rows, hd), F32),
            pltpu.VMEM((full_rows, hd), F32),
            pltpu.VMEM((8, hd), F32),
            pltpu.SemaphoreType.DMA((2, requests)),
        ],
        compiler_params=pltpu.CompilerParams(vmem_limit_bytes=48 * 2**20),
        name="attend",
    )(lists, x, mask, key_cache, value_cache)


def join_kernel(dims, where_ref, y_ref, o_ref):
    heads, splits, tl, group, hd = dims
    rows = tl * group
    span = hd // tl
    src = lax.broadcasted_iota(jnp.int32, (hd, tl * hd), 0)
    dst = lax.broadcasted_iota(jnp.int32, (hd, tl * hd), 1)
    pick = (src // span == dst // hd) & (src % span < 3)
    pick = pick.astype(F32).astype(BF16)
    first = where_ref[0]
    length = where_ref[1]
    for h in range(heads):
        stat = y_ref[h * splits : (h + 1) * splits, rows : rows + group, :]
        lse = jnp.dot(
            stat.reshape(splits * group, hd), pick, preferred_element_type=F32
        )
        for i in range(tl):
            one = lse[:, i * hd : (i + 1) * hd].reshape(splits, group, hd)
            high = jnp.max(one, 0, keepdims=True)
            w = jnp.exp2(one - high)
            o = y_ref[
                h * splits : (h + 1) * splits, i * group : (i + 1) * group, :
            ].astype(F32)
            res = jnp.sum(w * o, 0) / jnp.sum(w, 0)
            res = jnp.where(first + i < length, res, 0.0)
            o_ref[0, i, h * group : (h + 1) * group, :] = res.astype(BF16)


def join(where, y, dims):
    heads, splits, tl, group, hd = dims
    return pl.pallas_call(
        functools.partial(join_kernel, dims),
        out_shape=jax.ShapeDtypeStruct((1, tl, heads * group, hd), BF16),
        in_specs=[
            pl.BlockSpec(memory_space=pltpu.SMEM),
            pl.BlockSpec(memory_space=pltpu.VMEM),
        ],
        out_specs=pl.BlockSpec(memory_space=pltpu.VMEM),
        compiler_params=pltpu.CompilerParams(vmem_limit_bytes=16 * 2**20),
        name="join",
    )(where, y)


def per_device(
    queries,
    tree_keys,
    tree_values,
    key_cache,
    value_cache,
    page_request,
    page_index,
    ctx_len,
    tree_len,
    tree_mask,
):
    heads = lax.axis_size("kvh")
    splits = lax.axis_size("split")
    unused, tl, hq, hd = queries.shape
    group = hq // heads
    requests = ctx_len.shape[0]
    unused, pages, page, unused = key_cache.shape
    me = lax.axis_index("split").astype(jnp.int32)

    q = queries.reshape(tl, heads, group, hd).transpose(1, 0, 2, 3)
    x = jnp.concatenate(
        [
            q.reshape(heads, tl * group, hd),
            tree_keys[0].transpose(1, 0, 2),
            tree_values[0].transpose(1, 0, 2),
        ],
        1,
    )
    block = x.shape[1]
    x = jnp.broadcast_to(x[:, None], (heads, splits, block, hd))
    x = x.reshape(heads * splits, block, hd)
    x = lax.all_to_all(x, BOTH, 0, 0, tiled=True)

    meta = jnp.concatenate([page_request, page_index, ctx_len, tree_len, me[None]])
    dims = (requests, splits, tl, group, pages, page, hd)
    lists = prepare(meta, dims)
    y = attend(lists, x, tree_mask, key_cache, value_cache, dims)

    y = lax.all_to_all(y, BOTH, 0, 0, tiled=True)
    own = lax.axis_index("kvh")
    where = jnp.stack([me * tl, jnp.take(tree_len, own)])
    return join(where, y, (heads, splits, tl, group, hd))


def solution(mesh):
    shard = P("kvh", "split", None, None)
    return jax.shard_map(
        per_device,
        mesh=mesh,
        in_specs=(shard,) * 5 + (P("split"), P("split"), P(), P(), P()),
        out_specs=shard,
        check_vma=False,
    )
```

```python
import functools

import jax
import jax.numpy as jnp
from jax import lax
from jax.experimental import pallas as pl
from jax.experimental.pallas import tpu as pltpu
from jax.sharding import PartitionSpec as P

BOTH = ("kvh", "split")
NEG = -1e30
LOG2E = 1.4426950408889634
HUGE = 2.0**100
STEP = 16
TAIL = 4
CHUNK = 64
F32 = jnp.float32
BF16 = jnp.bfloat16

NT = (((1,), (1,)), ((), ()))


def column_bias(lims, page):
    col = lax.broadcasted_iota(jnp.int32, (1, page), 1)
    return jnp.concatenate([jnp.where(col < x, 0.0, NEG) for x in lims], 1)


def pack_kernel(dims, q_ref, tk_ref, tv_ref, o_ref, block, sems):
    heads, splits, tl, group, hd = dims
    tk = tk_ref[0].astype(F32)
    tv = tv_ref[0].astype(F32)
    for h in range(heads):
        for i in range(tl):
            block[h, i * group : (i + 1) * group, :] = q_ref[
                0, i, h * group : (h + 1) * group, :
            ]
        both = [t[i, h : h + 1] for t in (tk, tv) for i in range(tl)]
        block[h, tl * group :, :] = jnp.concatenate(both, 0).astype(BF16)
    copies = [
        pltpu.make_async_copy(block, o_ref.at[:, s], sems.at[s]) for s in range(splits)
    ]
    for c in copies:
        c.start()
    for c in copies:
        c.wait()


def pack(queries, tree_keys, tree_values, dims):
    heads, splits, tl, group, hd = dims
    rows = tl * group + 2 * tl
    vmem = pl.BlockSpec(memory_space=pltpu.VMEM)
    return pl.pallas_call(
        functools.partial(pack_kernel, dims),
        out_shape=jax.ShapeDtypeStruct((heads, splits, rows, hd), BF16),
        in_specs=[vmem, vmem, vmem],
        out_specs=pl.BlockSpec(memory_space=pltpu.HBM),
        scratch_shapes=[
            pltpu.VMEM((heads, rows, hd), BF16),
            pltpu.SemaphoreType.DMA((splits,)),
        ],
        compiler_params=pltpu.CompilerParams(vmem_limit_bytes=8 * 2**20),
        name="pack",
    )(queries, tree_keys, tree_values)


def prepare_kernel(dims, meta, lists):
    requests, splits, tl, group, pages, page, hd = dims
    i_ctx, i_tl = 2 * pages, 2 * pages + requests
    i_off, i_full, i_edge = pages, pages + requests + 1, pages + 2 * requests + 1
    i_len = pages + 3 * requests + 1
    for r in range(requests):
        lists[i_off + r] = 0
        lists[i_full + r] = 0
        lists[i_edge + r] = 0
        lists[i_len + r] = meta[i_tl + r]
    lists[i_len + requests] = meta[i_tl + requests]

    def tokens(p):
        r = meta[p]
        return r, meta[i_ctx + r] - meta[pages + p] * page

    def count(p, carry):
        r, lim = tokens(p)
        lists[p] = 0
        lists[i_full + r] += jnp.where(lim >= page, 1, 0)
        lists[i_edge + r] += jnp.where((lim > 0) & (lim < page), lim, 0)
        return carry

    lax.fori_loop(0, pages, count, 0)
    total = 0
    for r in range(requests):
        lists[i_off + r] = total
        total += lists[i_full + r] + jnp.where(lists[i_edge + r] > 0, 1, 0)
        lists[i_full + r] = 0
    lists[i_off + requests] = total

    def place(p, carry):
        r, lim = tokens(p)
        n = lists[i_full + r]
        whole = lim >= page

        @pl.when(whole)
        def _():
            lists[lists[i_off + r] + n] = p
            lists[i_full + r] = n + 1

        @pl.when((lim > 0) & (lim < page))
        def _():
            lists[lists[i_off + r + 1] - 1] = p

        return carry

    lax.fori_loop(0, pages, place, 0)


def prepare(meta, dims):
    requests, splits, tl, group, pages, page, hd = dims
    smem = pl.BlockSpec(memory_space=pltpu.SMEM)
    return pl.pallas_call(
        functools.partial(prepare_kernel, dims),
        out_shape=jax.ShapeDtypeStruct((pages + 4 * requests + 2,), jnp.int32),
        in_specs=[smem],
        out_specs=smem,
        compiler_params=pltpu.CompilerParams(vmem_limit_bytes=2**20),
        cost_estimate=pl.CostEstimate(
            flops=0, bytes_accessed=2**24, transcendentals=0
        ),
        name="prepare",
    )(meta)


def attn_kernel(
    dims,
    lists,
    x_ref,
    mask_ref,
    k_hbm,
    v_hbm,
    o_ref,
    k_ref,
    v_ref,
    m_s,
    l_s,
    acc,
    top,
    sems,
):
    requests, splits, tl, group, pages, page, hd = dims
    rows = tl * group
    full_rows = splits * rows
    scale = hd**-0.5 * LOG2E
    i_off, i_full, i_edge = pages, pages + requests + 1, pages + 2 * requests + 1
    i_tl = pages + 3 * requests + 1

    for r in range(requests):

        @pl.loop(lists[i_off + r], lists[i_off + r + 1])
        def _(slot):
            p = lists[slot]
            pltpu.make_async_copy(k_hbm.at[0, p], k_ref.at[slot], sems.at[0, r]).start()
            pltpu.make_async_copy(v_hbm.at[0, p], v_ref.at[slot], sems.at[1, r]).start()

    def arrive(r):
        n = lists[i_off + r + 1] - lists[i_off + r]

        @pl.when(n > 0)
        def _():
            at = pl.ds(0, n)
            for t, (src, dst) in enumerate(((k_hbm, k_ref), (v_hbm, v_ref))):
                pltpu.make_async_copy(src.at[0, at], dst.at[at], sems.at[t, r]).wait()

    me = lists[i_tl + requests]
    per = splits // requests
    tree_request = me // per
    part = me % per
    tree_rows = full_rows // per
    top[...] = jnp.zeros_like(top)

    def queries(r, count):
        blocks = count // rows
        return x_ref[pl.ds(r * splits, blocks), 0:rows, :].reshape(count, hd)

    def tree_page():
        first = pl.multiple_of(part * tree_rows, tree_rows)
        blk = tree_rows // rows
        q = x_ref[pl.ds(tree_request * splits + part * blk, blk), 0:rows, :]
        kv = x_ref[pl.ds(tree_request * splits, splits), rows : rows + 2 * tl, :]
        kv = kv.reshape(splits * 2 * tl, hd)
        wide = splits * 2 * tl
        values = pltpu.roll(kv.astype(F32), wide - tl, 0).astype(BF16)
        drafts = tree_rows // group
        mask = mask_ref[tree_request, pl.ds(part * drafts, drafts), :]
        tree = mask.shape[1]
        src = lax.broadcasted_iota(jnp.int32, (tree, wide), 0)
        dst = lax.broadcasted_iota(jnp.int32, (tree, wide), 1)
        pick = (src // tl == dst // (2 * tl)) & (src % tl == dst % (2 * tl))
        seen = jnp.dot(
            (mask == 1).astype(F32).astype(BF16),
            pick.astype(F32).astype(BF16),
            preferred_element_type=F32,
        )
        bias = jnp.where(seen > 0.5, 0.0, NEG)
        bias = jnp.broadcast_to(bias[:, None, :], (drafts, group, wide))
        s = lax.dot_general(q.reshape(tree_rows, hd), kv, NT, preferred_element_type=F32)
        return first, s + bias.reshape(tree_rows, wide), values

    def whole_block(r, start, nb):
        at = pl.ds(lists[i_off + r] + start, nb)
        return k_ref[at].reshape(nb * page, hd), v_ref[at].reshape(nb * page, hd)

    def pages_of(r):
        return lists[i_off + r + 1] - lists[i_off + r]

    def last_block(r, start, nb):
        n = pages_of(r)
        edge = lists[i_edge + r]
        ids, lims = [], []
        for j in range(nb):
            at = start + j
            ids.append(lists[i_off + r] + jnp.minimum(at, n - 1))
            lims.append(
                jnp.where(at < lists[i_full + r], page, jnp.where(at < n, edge, 0))
            )
        k = jnp.concatenate([k_ref[i] for i in ids], 0)
        v = jnp.concatenate([v_ref[i] for i in ids], 0)
        return k, v, column_bias(lims, page)

    def add(at, where, s, v):
        m = m_s[where, :]
        ps = [
            jnp.exp2(s[:, j : j + page] * scale - m) for j in range(0, s.shape[1], page)
        ]
        l_s[at, :] += functools.reduce(jnp.add, ps)
        p = jnp.concatenate([x.astype(BF16) for x in ps], 1)
        acc[at, :] += jnp.dot(p, v, preferred_element_type=F32)

    def add_online(at, where, s, v):
        old = m_s[where, :]
        new = jnp.maximum(old, jnp.max(s, 1, keepdims=True) * scale)
        m_s[where, :] = new
        fade = jnp.exp2(old - new)
        l_s[at, :] = l_s[at, :] * fade
        acc[at, :] = acc[at, :] * fade
        add(at, where, s, v)

    def finish(r, count):
        blocks = count // rows
        total = jnp.sum(l_s[0:count, :], 1, keepdims=True)
        total = jnp.broadcast_to(total, (count, hd))
        some = total > 0.0
        safe = jnp.where(some, total, 1.0)
        o = (acc[0:count, :] / safe).astype(BF16)
        o_ref[pl.ds(r * splits, blocks), 0:rows, :] = o.reshape(blocks, rows, hd)
        shift = m_s[pl.ds(r * full_rows, count), :]
        lse = jnp.where(some, shift + jnp.log2(safe), NEG)
        lse = lse.reshape(blocks, tl, group, hd)
        lane = lax.broadcasted_iota(jnp.int32, (1, 1, hd), 2)
        span = hd // tl
        both = lse[:, tl - 1]
        for i in range(tl - 2, -1, -1):
            both = jnp.where(lane < (i + 1) * span, lse[:, i], both)
        high = both.astype(BF16).astype(F32)
        mid = (both - high).astype(BF16).astype(F32)
        low = both - high - mid
        inner = lane % span
        stat = jnp.where(inner == 0, high, jnp.where(inner == 1, mid, low))
        o_ref[pl.ds(r * splits, blocks), rows : rows + group, :] = stat.astype(BF16)
        return total

    @pl.loop(0, requests)
    def _(r):
        for b in range(splits):
            for i in range(tl):
                block = r * splits + b
                q = x_ref[block, i * group : (i + 1) * group, :].astype(F32)
                key = x_ref[block, rows + i : rows + i + 1, :].astype(F32)
                s = jnp.sum(q * key, 1, keepdims=True) * scale
                at = pl.multiple_of(block * rows + i * group, group)
                m_s[pl.ds(at, group), :] = jnp.broadcast_to(s, (group, hd))

    def rows_of(r, first, count):
        return pl.ds(pl.multiple_of(r * full_rows + first, 8), count)

    def request(r, count):
        at = slice(0, count)
        where = rows_of(r, 0, count)
        l_s[...] = jnp.zeros_like(l_s)
        acc[...] = jnp.zeros_like(acc)

        @pl.when(r == tree_request)
        def _():
            first, s, v = tree_page()
            add(pl.ds(first, tree_rows), rows_of(r, first, tree_rows), s, v)

        q = queries(r, count)

        def take(start, nb):
            k, v = whole_block(r, start, nb)
            add(at, where, lax.dot_general(q, k, NT, preferred_element_type=F32), v)

        whole = lists[i_full + r] // STEP

        @pl.loop(0, whole)
        def _(b):
            take(b * STEP, STEP)

        start = whole * STEP
        quarters = (pages_of(r) - start + TAIL - 1) // TAIL
        for c in range(1, STEP // TAIL + 1):

            @pl.when(quarters == c)
            def _(c=c):
                k, v, bias = last_block(r, start, c * TAIL)
                s = lax.dot_general(q, k, NT, preferred_element_type=F32)
                add(at, where, s + bias, v)

        total = finish(r, count)
        high = functools.reduce(
            jnp.maximum, [total[j : j + 8] for j in range(0, count, 8)]
        )
        top[...] = jnp.maximum(top[...], high)

    def request_online(r):
        at = slice(0, full_rows)
        where = rows_of(r, 0, full_rows)
        m_s[where, :] = jnp.full((full_rows, hd), NEG, F32)
        l_s[...] = jnp.zeros_like(l_s)
        acc[...] = jnp.zeros_like(acc)

        @pl.when(r == tree_request)
        def _():
            first, s, v = tree_page()
            add_online(pl.ds(first, tree_rows), rows_of(r, first, tree_rows), s, v)

        q = queries(r, full_rows)

        @pl.loop(0, (pages_of(r) + 1) // 2)
        def _(b):
            k, v, bias = last_block(r, b * 2, 2)
            s = lax.dot_general(q, k, NT, preferred_element_type=F32)
            add_online(at, where, s + bias, v)

        finish(r, full_rows)

    @pl.loop(0, requests)
    def _(r):
        arrive(r)
        chunks = (lists[i_tl + r] * group + CHUNK - 1) // CHUNK
        for c in range(2, full_rows // CHUNK + 1):

            @pl.when((chunks == c) | ((c == 2) & (chunks < 2)))
            def _():
                request(r, c * CHUNK)

    @pl.when(jnp.logical_not(jnp.max(top[...]) < HUGE))
    def _():
        @pl.loop(0, requests)
        def _(r):
            request_online(r)


def attend(lists, x, mask, key_cache, value_cache, dims):
    requests, splits, tl, group, pages, page, hd = dims
    full_rows = splits * tl * group
    smem = pl.BlockSpec(memory_space=pltpu.SMEM)
    vmem = pl.BlockSpec(memory_space=pltpu.VMEM)
    hbm = pl.BlockSpec(memory_space=pltpu.HBM)
    return pl.pallas_call(
        functools.partial(attn_kernel, dims),
        out_shape=jax.ShapeDtypeStruct(x.shape, BF16),
        in_specs=[smem, vmem, vmem, hbm, hbm],
        out_specs=vmem,
        scratch_shapes=[
            pltpu.VMEM((pages, page, hd), BF16),
            pltpu.VMEM((pages, page, hd), BF16),
            pltpu.VMEM((requests * full_rows, hd), F32),
            pltpu.VMEM((full_rows, hd), F32),
            pltpu.VMEM((full_rows, hd), F32),
            pltpu.VMEM((8, hd), F32),
            pltpu.SemaphoreType.DMA((2, requests)),
        ],
        compiler_params=pltpu.CompilerParams(vmem_limit_bytes=48 * 2**20),
        name="attend",
    )(lists, x, mask, key_cache, value_cache)


def join_kernel(dims, where_ref, y_ref, o_ref):
    heads, splits, tl, group, hd = dims
    rows = tl * group
    span = hd // tl
    src = lax.broadcasted_iota(jnp.int32, (hd, tl * hd), 0)
    dst = lax.broadcasted_iota(jnp.int32, (hd, tl * hd), 1)
    pick = (src // span == dst // hd) & (src % span < 3)
    pick = pick.astype(F32).astype(BF16)
    first = where_ref[0]
    length = where_ref[1]
    for h in range(heads):
        stat = y_ref[h * splits : (h + 1) * splits, rows : rows + group, :]
        lse = jnp.dot(
            stat.reshape(splits * group, hd), pick, preferred_element_type=F32
        )
        for i in range(tl):
            one = lse[:, i * hd : (i + 1) * hd].reshape(splits, group, hd)
            high = jnp.max(one, 0, keepdims=True)
            w = jnp.exp2(one - high)
            o = y_ref[
                h * splits : (h + 1) * splits, i * group : (i + 1) * group, :
            ].astype(F32)
            res = jnp.sum(w * o, 0) / jnp.sum(w, 0)
            res = jnp.where(first + i < length, res, 0.0)
            o_ref[0, i, h * group : (h + 1) * group, :] = res.astype(BF16)


def join(where, y, dims):
    heads, splits, tl, group, hd = dims
    return pl.pallas_call(
        functools.partial(join_kernel, dims),
        out_shape=jax.ShapeDtypeStruct((1, tl, heads * group, hd), BF16),
        in_specs=[
            pl.BlockSpec(memory_space=pltpu.SMEM),
            pl.BlockSpec(memory_space=pltpu.VMEM),
        ],
        out_specs=pl.BlockSpec(memory_space=pltpu.VMEM),
        compiler_params=pltpu.CompilerParams(vmem_limit_bytes=16 * 2**20),
        name="join",
    )(where, y)


def per_device(
    queries,
    tree_keys,
    tree_values,
    key_cache,
    value_cache,
    page_request,
    page_index,
    ctx_len,
    tree_len,
    tree_mask,
):
    heads = lax.axis_size("kvh")
    splits = lax.axis_size("split")
    unused, tl, hq, hd = queries.shape
    group = hq // heads
    requests = ctx_len.shape[0]
    unused, pages, page, unused = key_cache.shape
    me = lax.axis_index("split").astype(jnp.int32)

    x = pack(queries, tree_keys, tree_values, (heads, splits, tl, group, hd))
    x = x.reshape((heads * splits,) + x.shape[2:])
    x = lax.all_to_all(x, BOTH, 0, 0, tiled=True)

    meta = jnp.concatenate([page_request, page_index, ctx_len, tree_len, me[None]])
    dims = (requests, splits, tl, group, pages, page, hd)
    lists = prepare(meta, dims)
    y = attend(lists, x, tree_mask, key_cache, value_cache, dims)

    y = lax.all_to_all(y, BOTH, 0, 0, tiled=True)
    own = lax.axis_index("kvh")
    where = jnp.stack([me * tl, jnp.take(tree_len, own)])
    return join(where, y, (heads, splits, tl, group, hd))


def solution(mesh):
    shard = P("kvh", "split", None, None)
    return jax.shard_map(
        per_device,
        mesh=mesh,
        in_specs=(shard,) * 5 + (P("split"), P("split"), P(), P(), P()),
        out_specs=shard,
        check_vma=False,
    )
```

```python
import functools

import jax
import jax.numpy as jnp
from jax import lax
from jax.experimental import pallas as pl
from jax.experimental.pallas import tpu as pltpu
from jax.sharding import PartitionSpec as P

BOTH = ("kvh", "split")
NEG = -1e30
LOG2E = 1.4426950408889634
HUGE = 2.0**100
TINY = 2.0**-120
STEP = 16
TAIL = 4
CHUNK = 64
F32 = jnp.float32
BF16 = jnp.bfloat16

NT = (((1,), (1,)), ((), ()))


def column_bias(lims, page):
    col = lax.broadcasted_iota(jnp.int32, (1, page), 1)
    return jnp.concatenate([jnp.where(col < x, 0.0, NEG) for x in lims], 1)


def pack_kernel(dims, q_hbm, tk_hbm, tv_hbm, o_ref, q_ref, tk_ref, tv_ref, block, sems):
    heads, splits, tl, group, hd = dims
    pairs = ((q_hbm, q_ref), (tk_hbm, tk_ref), (tv_hbm, tv_ref))
    arrivals = [
        pltpu.make_async_copy(src.at[0], dst, sems.at[splits + t])
        for t, (src, dst) in enumerate(pairs)
    ]
    for c in arrivals:
        c.start()
    for c in arrivals:
        c.wait()
    tk = tk_ref[...].astype(F32)
    tv = tv_ref[...].astype(F32)
    for h in range(heads):
        for i in range(tl):
            block[h, i * group : (i + 1) * group, :] = q_ref[
                i, h * group : (h + 1) * group, :
            ]
        both = [t[i, h : h + 1] for t in (tk, tv) for i in range(tl)]
        block[h, tl * group :, :] = jnp.concatenate(both, 0).astype(BF16)
    copies = [
        pltpu.make_async_copy(block, o_ref.at[:, s], sems.at[s]) for s in range(splits)
    ]
    for c in copies:
        c.start()
    for c in copies:
        c.wait()


def pack(queries, tree_keys, tree_values, dims):
    heads, splits, tl, group, hd = dims
    rows = tl * group + 2 * tl
    hbm = pl.BlockSpec(memory_space=pltpu.HBM)
    return pl.pallas_call(
        functools.partial(pack_kernel, dims),
        out_shape=jax.ShapeDtypeStruct((heads, splits, rows, hd), BF16),
        in_specs=[hbm, hbm, hbm],
        out_specs=hbm,
        scratch_shapes=[
            pltpu.VMEM((tl, heads * group, hd), BF16),
            pltpu.VMEM((tl, heads, hd), BF16),
            pltpu.VMEM((tl, heads, hd), BF16),
            pltpu.VMEM((heads, rows, hd), BF16),
            pltpu.SemaphoreType.DMA((splits + 3,)),
        ],
        compiler_params=pltpu.CompilerParams(vmem_limit_bytes=8 * 2**20),
        name="pack",
    )(queries, tree_keys, tree_values)


def prepare_kernel(dims, meta, lists):
    requests, splits, tl, group, pages, page, hd = dims
    i_ctx, i_tl = 2 * pages, 2 * pages + requests
    i_off, i_full, i_edge = pages, pages + requests + 1, pages + 2 * requests + 1
    i_len = pages + 3 * requests + 1
    for r in range(requests):
        lists[i_off + r] = 0
        lists[i_full + r] = 0
        lists[i_edge + r] = 0
        lists[i_len + r] = meta[i_tl + r]
    lists[i_len + requests] = meta[i_tl + requests]

    def tokens(p):
        r = meta[p]
        return r, meta[i_ctx + r] - meta[pages + p] * page

    def count(p, carry):
        r, lim = tokens(p)
        lists[p] = 0
        lists[i_full + r] += jnp.where(lim >= page, 1, 0)
        lists[i_edge + r] += jnp.where((lim > 0) & (lim < page), lim, 0)
        return carry

    lax.fori_loop(0, pages, count, 0)
    total = 0
    for r in range(requests):
        lists[i_off + r] = total
        total += lists[i_full + r] + jnp.where(lists[i_edge + r] > 0, 1, 0)
        lists[i_full + r] = 0
    lists[i_off + requests] = total

    def place(p, carry):
        r, lim = tokens(p)
        n = lists[i_full + r]
        whole = lim >= page

        @pl.when(whole)
        def _():
            lists[lists[i_off + r] + n] = p
            lists[i_full + r] = n + 1

        @pl.when((lim > 0) & (lim < page))
        def _():
            lists[lists[i_off + r + 1] - 1] = p

        return carry

    lax.fori_loop(0, pages, place, 0)


def prepare(meta, dims):
    requests, splits, tl, group, pages, page, hd = dims
    smem = pl.BlockSpec(memory_space=pltpu.SMEM)
    return pl.pallas_call(
        functools.partial(prepare_kernel, dims),
        out_shape=jax.ShapeDtypeStruct((pages + 4 * requests + 2,), jnp.int32),
        in_specs=[smem],
        out_specs=smem,
        compiler_params=pltpu.CompilerParams(vmem_limit_bytes=2**20),
        cost_estimate=pl.CostEstimate(
            flops=0, bytes_accessed=2**24, transcendentals=0
        ),
        name="prepare",
    )(meta)


def attn_kernel(
    dims,
    lists,
    x_ref,
    mask_ref,
    k_hbm,
    v_hbm,
    o_hbm,
    o_ref,
    k_ref,
    v_ref,
    m_s,
    l_s,
    acc,
    top,
    sems,
    out_sems,
):
    requests, splits, tl, group, pages, page, hd = dims
    rows = tl * group
    full_rows = splits * rows
    scale = hd**-0.5 * LOG2E
    i_off, i_full, i_edge = pages, pages + requests + 1, pages + 2 * requests + 1
    i_tl = pages + 3 * requests + 1

    for r in range(requests):

        @pl.loop(lists[i_off + r], lists[i_off + r + 1])
        def _(slot):
            p = lists[slot]
            pltpu.make_async_copy(k_hbm.at[0, p], k_ref.at[slot], sems.at[0, r]).start()
            pltpu.make_async_copy(v_hbm.at[0, p], v_ref.at[slot], sems.at[1, r]).start()

    def arrive(r):
        n = lists[i_off + r + 1] - lists[i_off + r]

        @pl.when(n > 0)
        def _():
            at = pl.ds(0, n)
            for t, (src, dst) in enumerate(((k_hbm, k_ref), (v_hbm, v_ref))):
                pltpu.make_async_copy(src.at[0, at], dst.at[at], sems.at[t, r]).wait()

    me = lists[i_tl + requests]
    per = splits // requests
    tree_request = me // per
    part = me % per
    tree_rows = full_rows // per
    top[...] = jnp.zeros_like(top)

    def queries(r, count):
        blocks = count // rows
        return x_ref[pl.ds(r * splits, blocks), 0:rows, :].reshape(count, hd)

    def tree_page():
        first = pl.multiple_of(part * tree_rows, tree_rows)
        blk = tree_rows // rows
        q = x_ref[pl.ds(tree_request * splits + part * blk, blk), 0:rows, :]
        kv = x_ref[pl.ds(tree_request * splits, splits), rows : rows + 2 * tl, :]
        kv = kv.reshape(splits * 2 * tl, hd)
        wide = splits * 2 * tl
        values = pltpu.roll(kv.astype(F32), wide - tl, 0).astype(BF16)
        drafts = tree_rows // group
        mask = mask_ref[tree_request, pl.ds(part * drafts, drafts), :]
        tree = mask.shape[1]
        src = lax.broadcasted_iota(jnp.int32, (tree, wide), 0)
        dst = lax.broadcasted_iota(jnp.int32, (tree, wide), 1)
        pick = (src // tl == dst // (2 * tl)) & (src % tl == dst % (2 * tl))
        seen = jnp.dot(
            (mask == 1).astype(F32).astype(BF16),
            pick.astype(F32).astype(BF16),
            preferred_element_type=F32,
        )
        bias = jnp.where(seen > 0.5, 0.0, NEG)
        bias = jnp.broadcast_to(bias[:, None, :], (drafts, group, wide))
        s = lax.dot_general(q.reshape(tree_rows, hd), kv, NT, preferred_element_type=F32)
        return first, s + bias.reshape(tree_rows, wide), values

    def whole_block(r, start, nb):
        at = pl.ds(lists[i_off + r] + start, nb)
        return k_ref[at].reshape(nb * page, hd), v_ref[at].reshape(nb * page, hd)

    def pages_of(r):
        return lists[i_off + r + 1] - lists[i_off + r]

    def last_block(r, start, nb):
        n = pages_of(r)
        edge = lists[i_edge + r]
        ids, lims = [], []
        for j in range(nb):
            at = start + j
            ids.append(lists[i_off + r] + jnp.minimum(at, n - 1))
            lims.append(
                jnp.where(at < lists[i_full + r], page, jnp.where(at < n, edge, 0))
            )
        k = jnp.concatenate([k_ref[i] for i in ids], 0)
        v = jnp.concatenate([v_ref[i] for i in ids], 0)
        return k, v, column_bias(lims, page)

    def add(at, where, s, v):
        m = m_s[where, :]
        ps = [
            jnp.exp2(s[:, j : j + page] * scale - m) for j in range(0, s.shape[1], page)
        ]
        l_s[at, :] += functools.reduce(jnp.add, ps)
        p = jnp.concatenate([x.astype(BF16) for x in ps], 1)
        acc[at, :] += jnp.dot(p, v, preferred_element_type=F32)

    def add_online(at, where, s, v):
        old = m_s[where, :]
        new = jnp.maximum(old, jnp.max(s, 1, keepdims=True) * scale)
        m_s[where, :] = new
        fade = jnp.exp2(old - new)
        l_s[at, :] = l_s[at, :] * fade
        acc[at, :] = acc[at, :] * fade
        add(at, where, s, v)

    def finish(r, count):
        blocks = count // rows
        total = jnp.sum(l_s[0:count, :], 1, keepdims=True)
        total = jnp.broadcast_to(total, (count, hd))
        o = (acc[0:count, :] / jnp.maximum(total, TINY)).astype(BF16)
        o_ref[pl.ds(r * splits, blocks), 0:rows, :] = o.reshape(blocks, rows, hd)
        lane = lax.broadcasted_iota(jnp.int32, (1, 1, hd), 2)
        span = hd // tl

        def by_lane(x):
            x = x.reshape(blocks, tl, group, hd)
            out = x[:, tl - 1]
            for i in range(tl - 2, -1, -1):
                out = jnp.where(lane < (i + 1) * span, x[:, i], out)
            return out

        sums = by_lane(total)
        shift = by_lane(m_s[pl.ds(r * full_rows, count), :])
        both = jnp.where(sums > 0.0, shift + jnp.log2(jnp.maximum(sums, TINY)), NEG)
        high = both.astype(BF16).astype(F32)
        mid = (both - high).astype(BF16).astype(F32)
        low = both - high - mid
        inner = lane % span
        stat = jnp.where(inner == 0, high, jnp.where(inner == 1, mid, low))
        o_ref[pl.ds(r * splits, blocks), rows : rows + group, :] = stat.astype(BF16)
        return total

    @pl.loop(0, requests)
    def _(r):
        for b in range(splits):
            for i in range(tl):
                block = r * splits + b
                q = x_ref[block, i * group : (i + 1) * group, :].astype(F32)
                key = x_ref[block, rows + i : rows + i + 1, :].astype(F32)
                s = jnp.sum(q * key, 1, keepdims=True) * scale
                at = pl.multiple_of(block * rows + i * group, group)
                m_s[pl.ds(at, group), :] = jnp.broadcast_to(s, (group, hd))

    def send(r):
        at = pl.ds(r * splits, splits)
        return pltpu.make_async_copy(o_ref.at[at], o_hbm.at[at], out_sems.at[r])

    def rows_of(r, first, count):
        return pl.ds(pl.multiple_of(r * full_rows + first, 8), count)

    def request(r, count):
        at = slice(0, count)
        where = rows_of(r, 0, count)
        l_s[...] = jnp.zeros_like(l_s)
        acc[...] = jnp.zeros_like(acc)

        @pl.when(r == tree_request)
        def _():
            first, s, v = tree_page()
            add(pl.ds(first, tree_rows), rows_of(r, first, tree_rows), s, v)

        q = queries(r, count)

        def take(start, nb):
            k, v = whole_block(r, start, nb)
            add(at, where, lax.dot_general(q, k, NT, preferred_element_type=F32), v)

        whole = lists[i_full + r] // STEP

        @pl.loop(0, whole)
        def _(b):
            take(b * STEP, STEP)

        start = whole * STEP
        quarters = (pages_of(r) - start + TAIL - 1) // TAIL
        for c in range(1, STEP // TAIL + 1):

            @pl.when(quarters == c)
            def _(c=c):
                k, v, bias = last_block(r, start, c * TAIL)
                s = lax.dot_general(q, k, NT, preferred_element_type=F32)
                add(at, where, s + bias, v)

        total = finish(r, count)
        high = functools.reduce(
            jnp.maximum, [total[j : j + 8] for j in range(0, count, 8)]
        )
        top[...] = jnp.maximum(top[...], high)

    def request_online(r):
        at = slice(0, full_rows)
        where = rows_of(r, 0, full_rows)
        m_s[where, :] = jnp.full((full_rows, hd), NEG, F32)
        l_s[...] = jnp.zeros_like(l_s)
        acc[...] = jnp.zeros_like(acc)

        @pl.when(r == tree_request)
        def _():
            first, s, v = tree_page()
            add_online(pl.ds(first, tree_rows), rows_of(r, first, tree_rows), s, v)

        q = queries(r, full_rows)

        @pl.loop(0, (pages_of(r) + 1) // 2)
        def _(b):
            k, v, bias = last_block(r, b * 2, 2)
            s = lax.dot_general(q, k, NT, preferred_element_type=F32)
            add_online(at, where, s + bias, v)

        finish(r, full_rows)

    @pl.loop(0, requests)
    def _(r):
        arrive(r)
        chunks = (lists[i_tl + r] * group + CHUNK - 1) // CHUNK
        for c in range(2, full_rows // CHUNK + 1):

            @pl.when((chunks == c) | ((c == 2) & (chunks < 2)))
            def _():
                request(r, c * CHUNK)

        send(r).start()

    for r in range(requests):
        send(r).wait()

    @pl.when(jnp.logical_not(jnp.max(top[...]) < HUGE))
    def _():
        @pl.loop(0, requests)
        def _(r):
            request_online(r)
            send(r).start()
            send(r).wait()


def attend(lists, x, mask, key_cache, value_cache, dims):
    requests, splits, tl, group, pages, page, hd = dims
    full_rows = splits * tl * group
    smem = pl.BlockSpec(memory_space=pltpu.SMEM)
    vmem = pl.BlockSpec(memory_space=pltpu.VMEM)
    hbm = pl.BlockSpec(memory_space=pltpu.HBM)
    return pl.pallas_call(
        functools.partial(attn_kernel, dims),
        out_shape=jax.ShapeDtypeStruct(x.shape, BF16),
        in_specs=[smem, vmem, vmem, hbm, hbm],
        out_specs=hbm,
        scratch_shapes=[
            pltpu.VMEM(x.shape, BF16),
            pltpu.VMEM((pages, page, hd), BF16),
            pltpu.VMEM((pages, page, hd), BF16),
            pltpu.VMEM((requests * full_rows, hd), F32),
            pltpu.VMEM((full_rows, hd), F32),
            pltpu.VMEM((full_rows, hd), F32),
            pltpu.VMEM((8, hd), F32),
            pltpu.SemaphoreType.DMA((2, requests)),
            pltpu.SemaphoreType.DMA((requests,)),
        ],
        compiler_params=pltpu.CompilerParams(vmem_limit_bytes=48 * 2**20),
        name="attend",
    )(lists, x, mask, key_cache, value_cache)


def join_kernel(dims, where_ref, y_ref, o_ref):
    heads, splits, tl, group, hd = dims
    rows = tl * group
    span = hd // tl
    src = lax.broadcasted_iota(jnp.int32, (hd, tl * hd), 0)
    dst = lax.broadcasted_iota(jnp.int32, (hd, tl * hd), 1)
    pick = (src // span == dst // hd) & (src % span < 3)
    pick = pick.astype(F32).astype(BF16)
    first = where_ref[0]
    length = where_ref[1]
    for h in range(heads):
        stat = y_ref[h * splits : (h + 1) * splits, rows : rows + group, :]
        lse = jnp.dot(
            stat.reshape(splits * group, hd), pick, preferred_element_type=F32
        )
        for i in range(tl):
            one = lse[:, i * hd : (i + 1) * hd].reshape(splits, group, hd)
            high = jnp.max(one, 0, keepdims=True)
            w = jnp.exp2(one - high)
            o = y_ref[
                h * splits : (h + 1) * splits, i * group : (i + 1) * group, :
            ].astype(F32)
            res = jnp.sum(w * o, 0) / jnp.sum(w, 0)
            res = jnp.where(first + i < length, res, 0.0)
            o_ref[0, i, h * group : (h + 1) * group, :] = res.astype(BF16)


def join(where, y, dims):
    heads, splits, tl, group, hd = dims
    return pl.pallas_call(
        functools.partial(join_kernel, dims),
        out_shape=jax.ShapeDtypeStruct((1, tl, heads * group, hd), BF16),
        in_specs=[
            pl.BlockSpec(memory_space=pltpu.SMEM),
            pl.BlockSpec(memory_space=pltpu.VMEM),
        ],
        out_specs=pl.BlockSpec(memory_space=pltpu.VMEM),
        compiler_params=pltpu.CompilerParams(vmem_limit_bytes=16 * 2**20),
        name="join",
    )(where, y)


def per_device(
    queries,
    tree_keys,
    tree_values,
    key_cache,
    value_cache,
    page_request,
    page_index,
    ctx_len,
    tree_len,
    tree_mask,
):
    heads = lax.axis_size("kvh")
    splits = lax.axis_size("split")
    unused, tl, hq, hd = queries.shape
    group = hq // heads
    requests = ctx_len.shape[0]
    unused, pages, page, unused = key_cache.shape
    me = lax.axis_index("split").astype(jnp.int32)

    x = pack(queries, tree_keys, tree_values, (heads, splits, tl, group, hd))
    x = x.reshape((heads * splits,) + x.shape[2:])
    x = lax.all_to_all(x, BOTH, 0, 0, tiled=True)

    meta = jnp.concatenate([page_request, page_index, ctx_len, tree_len, me[None]])
    dims = (requests, splits, tl, group, pages, page, hd)
    lists = prepare(meta, dims)
    y = attend(lists, x, tree_mask, key_cache, value_cache, dims)

    y = lax.all_to_all(y, BOTH, 0, 0, tiled=True)
    own = lax.axis_index("kvh")
    where = jnp.stack([me * tl, jnp.take(tree_len, own)])
    return join(where, y, (heads, splits, tl, group, hd))


def solution(mesh):
    shard = P("kvh", "split", None, None)
    return jax.shard_map(
        per_device,
        mesh=mesh,
        in_specs=(shard,) * 5 + (P("split"), P("split"), P(), P(), P()),
        out_specs=shard,
        check_vma=False,
    )
```

```python
import functools

import jax
import jax.numpy as jnp
from jax import lax
from jax.experimental import pallas as pl
from jax.experimental.pallas import tpu as pltpu
from jax.sharding import PartitionSpec as P

BOTH = ("kvh", "split")
NEG = -1e30
LOG2E = 1.4426950408889634
HUGE = 2.0**100
TINY = 2.0**-120
STEP = 16
TAIL = 4
CHUNK = 64
F32 = jnp.float32
BF16 = jnp.bfloat16

NT = (((1,), (1,)), ((), ()))


def column_bias(lims, page):
    col = lax.broadcasted_iota(jnp.int32, (1, page), 1)
    return jnp.concatenate([jnp.where(col < x, 0.0, NEG) for x in lims], 1)


def pack_kernel(dims, q_hbm, tk_hbm, tv_hbm, o_ref, q_ref, tk_ref, tv_ref, block, sems):
    heads, splits, tl, group, hd = dims
    pairs = ((q_hbm, q_ref), (tk_hbm, tk_ref), (tv_hbm, tv_ref))
    arrivals = [
        pltpu.make_async_copy(src.at[0], dst, sems.at[splits + t])
        for t, (src, dst) in enumerate(pairs)
    ]
    for c in arrivals:
        c.start()
    for c in arrivals:
        c.wait()
    tk = tk_ref[...].astype(F32)
    tv = tv_ref[...].astype(F32)
    for h in range(heads):
        for i in range(tl):
            block[h, i * group : (i + 1) * group, :] = q_ref[
                i, h * group : (h + 1) * group, :
            ]
        both = [t[i, h : h + 1] for t in (tk, tv) for i in range(tl)]
        block[h, tl * group :, :] = jnp.concatenate(both, 0).astype(BF16)
    copies = [
        pltpu.make_async_copy(block, o_ref.at[:, s], sems.at[s]) for s in range(splits)
    ]
    for c in copies:
        c.start()
    for c in copies:
        c.wait()


def pack(queries, tree_keys, tree_values, dims):
    heads, splits, tl, group, hd = dims
    rows = tl * group + 2 * tl
    hbm = pl.BlockSpec(memory_space=pltpu.HBM)
    return pl.pallas_call(
        functools.partial(pack_kernel, dims),
        out_shape=jax.ShapeDtypeStruct((heads, splits, rows, hd), BF16),
        in_specs=[hbm, hbm, hbm],
        out_specs=hbm,
        scratch_shapes=[
            pltpu.VMEM((tl, heads * group, hd), BF16),
            pltpu.VMEM((tl, heads, hd), BF16),
            pltpu.VMEM((tl, heads, hd), BF16),
            pltpu.VMEM((heads, rows, hd), BF16),
            pltpu.SemaphoreType.DMA((splits + 3,)),
        ],
        name="pack",
    )(queries, tree_keys, tree_values)


def prepare_kernel(dims, meta, lists):
    requests, splits, tl, group, pages, page, hd = dims
    i_ctx, i_tl = 2 * pages, 2 * pages + requests
    i_off, i_full, i_edge = pages, pages + requests + 1, pages + 2 * requests + 1
    i_len = pages + 3 * requests + 1
    for r in range(requests):
        lists[i_off + r] = 0
        lists[i_full + r] = 0
        lists[i_edge + r] = 0
        lists[i_len + r] = meta[i_tl + r]
    lists[i_len + requests] = meta[i_tl + requests]

    def tokens(p):
        r = meta[p]
        return r, meta[i_ctx + r] - meta[pages + p] * page

    def count(p, carry):
        r, lim = tokens(p)
        lists[p] = 0
        lists[i_full + r] += jnp.where(lim >= page, 1, 0)
        lists[i_edge + r] += jnp.where((lim > 0) & (lim < page), lim, 0)
        return carry

    lax.fori_loop(0, pages, count, 0)
    total = 0
    for r in range(requests):
        lists[i_off + r] = total
        total += lists[i_full + r] + jnp.where(lists[i_edge + r] > 0, 1, 0)
        lists[i_full + r] = 0
    lists[i_off + requests] = total

    def place(p, carry):
        r, lim = tokens(p)
        n = lists[i_full + r]
        whole = lim >= page

        @pl.when(whole)
        def _():
            lists[lists[i_off + r] + n] = p
            lists[i_full + r] = n + 1

        @pl.when((lim > 0) & (lim < page))
        def _():
            lists[lists[i_off + r + 1] - 1] = p

        return carry

    lax.fori_loop(0, pages, place, 0)


def prepare(meta, dims):
    requests, splits, tl, group, pages, page, hd = dims
    smem = pl.BlockSpec(memory_space=pltpu.SMEM)
    return pl.pallas_call(
        functools.partial(prepare_kernel, dims),
        out_shape=jax.ShapeDtypeStruct((pages + 4 * requests + 2,), jnp.int32),
        in_specs=[smem],
        out_specs=smem,
        compiler_params=pltpu.CompilerParams(vmem_limit_bytes=2**20),
        cost_estimate=pl.CostEstimate(
            flops=0, bytes_accessed=2**24, transcendentals=0
        ),
        name="prepare",
    )(meta)


def attn_kernel(
    dims,
    lists,
    x_ref,
    mask_ref,
    k_hbm,
    v_hbm,
    o_hbm,
    o_ref,
    k_ref,
    v_ref,
    m_s,
    l_s,
    acc,
    top,
    sems,
    out_sems,
):
    requests, splits, tl, group, pages, page, hd = dims
    rows = tl * group
    full_rows = splits * rows
    scale = hd**-0.5 * LOG2E
    i_off, i_full, i_edge = pages, pages + requests + 1, pages + 2 * requests + 1
    i_tl = pages + 3 * requests + 1

    for r in range(requests):

        @pl.loop(lists[i_off + r], lists[i_off + r + 1])
        def _(slot):
            p = lists[slot]
            pltpu.make_async_copy(k_hbm.at[0, p], k_ref.at[slot], sems.at[0, r]).start()
            pltpu.make_async_copy(v_hbm.at[0, p], v_ref.at[slot], sems.at[1, r]).start()

    def arrive(r):
        n = lists[i_off + r + 1] - lists[i_off + r]

        @pl.when(n > 0)
        def _():
            at = pl.ds(0, n)
            for t, (src, dst) in enumerate(((k_hbm, k_ref), (v_hbm, v_ref))):
                pltpu.make_async_copy(src.at[0, at], dst.at[at], sems.at[t, r]).wait()

    me = lists[i_tl + requests]
    per = splits // requests
    tree_request = me // per
    part = me % per
    tree_rows = full_rows // per
    top[...] = jnp.zeros_like(top)

    def queries(r, count):
        blocks = count // rows
        return x_ref[pl.ds(r * splits, blocks), 0:rows, :].reshape(count, hd)

    def tree_page():
        first = pl.multiple_of(part * tree_rows, tree_rows)
        blk = tree_rows // rows
        q = x_ref[pl.ds(tree_request * splits + part * blk, blk), 0:rows, :]
        kv = x_ref[pl.ds(tree_request * splits, splits), rows : rows + 2 * tl, :]
        kv = kv.reshape(splits * 2 * tl, hd)
        wide = splits * 2 * tl
        values = pltpu.roll(kv.astype(F32), wide - tl, 0).astype(BF16)
        drafts = tree_rows // group
        mask = mask_ref[tree_request, pl.ds(part * drafts, drafts), :]
        tree = mask.shape[1]
        src = lax.broadcasted_iota(jnp.int32, (tree, wide), 0)
        dst = lax.broadcasted_iota(jnp.int32, (tree, wide), 1)
        pick = (src // tl == dst // (2 * tl)) & (src % tl == dst % (2 * tl))
        seen = jnp.dot(
            (mask == 1).astype(F32).astype(BF16),
            pick.astype(F32).astype(BF16),
            preferred_element_type=F32,
        )
        bias = jnp.where(seen > 0.5, 0.0, NEG)
        bias = jnp.broadcast_to(bias[:, None, :], (drafts, group, wide))
        s = lax.dot_general(q.reshape(tree_rows, hd), kv, NT, preferred_element_type=F32)
        return first, s + bias.reshape(tree_rows, wide), values

    def whole_block(r, start, nb):
        at = pl.ds(lists[i_off + r] + start, nb)
        return k_ref[at].reshape(nb * page, hd), v_ref[at].reshape(nb * page, hd)

    def pages_of(r):
        return lists[i_off + r + 1] - lists[i_off + r]

    def last_block(r, start, nb):
        n = pages_of(r)
        edge = lists[i_edge + r]
        ids, lims = [], []
        for j in range(nb):
            at = start + j
            ids.append(lists[i_off + r] + jnp.minimum(at, n - 1))
            lims.append(
                jnp.where(at < lists[i_full + r], page, jnp.where(at < n, edge, 0))
            )
        k = jnp.concatenate([k_ref[i] for i in ids], 0)
        v = jnp.concatenate([v_ref[i] for i in ids], 0)
        return k, v, column_bias(lims, page)

    def add(at, where, s, v):
        m = m_s[where, :]
        ps = [
            jnp.exp2(s[:, j : j + page] * scale - m) for j in range(0, s.shape[1], page)
        ]
        l_s[at, :] += functools.reduce(jnp.add, ps)
        p = jnp.concatenate([x.astype(BF16) for x in ps], 1)
        acc[at, :] += jnp.dot(p, v, preferred_element_type=F32)

    def add_online(at, where, s, v):
        old = m_s[where, :]
        new = jnp.maximum(old, jnp.max(s, 1, keepdims=True) * scale)
        m_s[where, :] = new
        fade = jnp.exp2(old - new)
        l_s[at, :] = l_s[at, :] * fade
        acc[at, :] = acc[at, :] * fade
        add(at, where, s, v)

    def finish(r, count):
        blocks = count // rows
        total = jnp.sum(l_s[0:count, :], 1, keepdims=True)
        total = jnp.broadcast_to(total, (count, hd))
        o = (acc[0:count, :] / jnp.maximum(total, TINY)).astype(BF16)
        o_ref[pl.ds(r * splits, blocks), 0:rows, :] = o.reshape(blocks, rows, hd)
        lane = lax.broadcasted_iota(jnp.int32, (1, 1, hd), 2)
        span = hd // tl

        def by_lane(x):
            x = x.reshape(blocks, tl, group, hd)
            out = x[:, tl - 1]
            for i in range(tl - 2, -1, -1):
                out = jnp.where(lane < (i + 1) * span, x[:, i], out)
            return out

        sums = by_lane(total)
        shift = by_lane(m_s[pl.ds(r * full_rows, count), :])
        both = jnp.where(sums > 0.0, shift + jnp.log2(jnp.maximum(sums, TINY)), NEG)
        high = both.astype(BF16).astype(F32)
        mid = (both - high).astype(BF16).astype(F32)
        low = both - high - mid
        inner = lane % span
        stat = jnp.where(inner == 0, high, jnp.where(inner == 1, mid, low))
        o_ref[pl.ds(r * splits, blocks), rows : rows + group, :] = stat.astype(BF16)
        return total

    @pl.loop(0, requests)
    def _(r):
        for b in range(splits):
            for i in range(tl):
                block = r * splits + b
                q = x_ref[block, i * group : (i + 1) * group, :].astype(F32)
                key = x_ref[block, rows + i : rows + i + 1, :].astype(F32)
                s = jnp.sum(q * key, 1, keepdims=True) * scale
                at = pl.multiple_of(block * rows + i * group, group)
                m_s[pl.ds(at, group), :] = jnp.broadcast_to(s, (group, hd))

    def send(r):
        at = pl.ds(r * splits, splits)
        return pltpu.make_async_copy(o_ref.at[at], o_hbm.at[at], out_sems.at[r])

    def rows_of(r, first, count):
        return pl.ds(pl.multiple_of(r * full_rows + first, 8), count)

    def request(r, count):
        at = slice(0, count)
        where = rows_of(r, 0, count)
        l_s[...] = jnp.zeros_like(l_s)
        acc[...] = jnp.zeros_like(acc)

        @pl.when(r == tree_request)
        def _():
            first, s, v = tree_page()
            add(pl.ds(first, tree_rows), rows_of(r, first, tree_rows), s, v)

        q = queries(r, count)

        def take(start, nb):
            k, v = whole_block(r, start, nb)
            add(at, where, lax.dot_general(q, k, NT, preferred_element_type=F32), v)

        whole = lists[i_full + r] // STEP

        @pl.loop(0, whole)
        def _(b):
            take(b * STEP, STEP)

        start = whole * STEP
        quarters = (pages_of(r) - start + TAIL - 1) // TAIL
        for c in range(1, STEP // TAIL + 1):

            @pl.when(quarters == c)
            def _(c=c):
                k, v, bias = last_block(r, start, c * TAIL)
                s = lax.dot_general(q, k, NT, preferred_element_type=F32)
                add(at, where, s + bias, v)

        total = finish(r, count)
        high = functools.reduce(
            jnp.maximum, [total[j : j + 8] for j in range(0, count, 8)]
        )
        top[...] = jnp.maximum(top[...], high)

    def request_online(r):
        at = slice(0, full_rows)
        where = rows_of(r, 0, full_rows)
        m_s[where, :] = jnp.full((full_rows, hd), NEG, F32)
        l_s[...] = jnp.zeros_like(l_s)
        acc[...] = jnp.zeros_like(acc)

        @pl.when(r == tree_request)
        def _():
            first, s, v = tree_page()
            add_online(pl.ds(first, tree_rows), rows_of(r, first, tree_rows), s, v)

        q = queries(r, full_rows)

        @pl.loop(0, (pages_of(r) + 1) // 2)
        def _(b):
            k, v, bias = last_block(r, b * 2, 2)
            s = lax.dot_general(q, k, NT, preferred_element_type=F32)
            add_online(at, where, s + bias, v)

        finish(r, full_rows)

    @pl.loop(0, requests)
    def _(r):
        arrive(r)
        chunks = (lists[i_tl + r] * group + CHUNK - 1) // CHUNK
        for c in range(2, full_rows // CHUNK + 1):

            @pl.when((chunks == c) | ((c == 2) & (chunks < 2)))
            def _():
                request(r, c * CHUNK)

        send(r).start()

    for r in range(requests):
        send(r).wait()

    @pl.when(jnp.logical_not(jnp.max(top[...]) < HUGE))
    def _():
        @pl.loop(0, requests)
        def _(r):
            request_online(r)
            send(r).start()
            send(r).wait()


def attend(lists, x, mask, key_cache, value_cache, dims):
    requests, splits, tl, group, pages, page, hd = dims
    full_rows = splits * tl * group
    smem = pl.BlockSpec(memory_space=pltpu.SMEM)
    vmem = pl.BlockSpec(memory_space=pltpu.VMEM)
    hbm = pl.BlockSpec(memory_space=pltpu.HBM)
    return pl.pallas_call(
        functools.partial(attn_kernel, dims),
        out_shape=jax.ShapeDtypeStruct(x.shape, BF16),
        in_specs=[smem, vmem, vmem, hbm, hbm],
        out_specs=hbm,
        scratch_shapes=[
            pltpu.VMEM(x.shape, BF16),
            pltpu.VMEM((pages, page, hd), BF16),
            pltpu.VMEM((pages, page, hd), BF16),
            pltpu.VMEM((requests * full_rows, hd), F32),
            pltpu.VMEM((full_rows, hd), F32),
            pltpu.VMEM((full_rows, hd), F32),
            pltpu.VMEM((8, hd), F32),
            pltpu.SemaphoreType.DMA((2, requests)),
            pltpu.SemaphoreType.DMA((requests,)),
        ],
        compiler_params=pltpu.CompilerParams(vmem_limit_bytes=48 * 2**20),
        name="attend",
    )(lists, x, mask, key_cache, value_cache)


def join_kernel(dims, where_ref, y_ref, o_ref):
    heads, splits, tl, group, hd = dims
    rows = tl * group
    span = hd // tl
    src = lax.broadcasted_iota(jnp.int32, (hd, tl * hd), 0)
    dst = lax.broadcasted_iota(jnp.int32, (hd, tl * hd), 1)
    pick = (src // span == dst // hd) & (src % span < 3)
    pick = pick.astype(F32).astype(BF16)
    first = where_ref[0]
    length = where_ref[1]
    for h in range(heads):
        stat = y_ref[h * splits : (h + 1) * splits, rows : rows + group, :]
        lse = jnp.dot(
            stat.reshape(splits * group, hd), pick, preferred_element_type=F32
        )
        for i in range(tl):
            one = lse[:, i * hd : (i + 1) * hd].reshape(splits, group, hd)
            high = jnp.max(one, 0, keepdims=True)
            w = jnp.exp2(one - high)
            o = y_ref[
                h * splits : (h + 1) * splits, i * group : (i + 1) * group, :
            ].astype(F32)
            res = jnp.sum(w * o, 0) / jnp.sum(w, 0)
            res = jnp.where(first + i < length, res, 0.0)
            o_ref[0, i, h * group : (h + 1) * group, :] = res.astype(BF16)


def join(where, y, dims):
    heads, splits, tl, group, hd = dims
    return pl.pallas_call(
        functools.partial(join_kernel, dims),
        out_shape=jax.ShapeDtypeStruct((1, tl, heads * group, hd), BF16),
        in_specs=[
            pl.BlockSpec(memory_space=pltpu.SMEM),
            pl.BlockSpec(memory_space=pltpu.VMEM),
        ],
        out_specs=pl.BlockSpec(memory_space=pltpu.VMEM),
        compiler_params=pltpu.CompilerParams(vmem_limit_bytes=16 * 2**20),
        name="join",
    )(where, y)


def per_device(
    queries,
    tree_keys,
    tree_values,
    key_cache,
    value_cache,
    page_request,
    page_index,
    ctx_len,
    tree_len,
    tree_mask,
):
    heads = lax.axis_size("kvh")
    splits = lax.axis_size("split")
    unused, tl, hq, hd = queries.shape
    group = hq // heads
    requests = ctx_len.shape[0]
    unused, pages, page, unused = key_cache.shape
    me = lax.axis_index("split").astype(jnp.int32)

    x = pack(queries, tree_keys, tree_values, (heads, splits, tl, group, hd))
    x = x.reshape((heads * splits,) + x.shape[2:])
    x = lax.all_to_all(x, BOTH, 0, 0, tiled=True)

    meta = jnp.concatenate([page_request, page_index, ctx_len, tree_len, me[None]])
    dims = (requests, splits, tl, group, pages, page, hd)
    lists = prepare(meta, dims)
    y = attend(lists, x, tree_mask, key_cache, value_cache, dims)

    y = lax.all_to_all(y, BOTH, 0, 0, tiled=True)
    own = lax.axis_index("kvh")
    where = jnp.stack([me * tl, jnp.take(tree_len, own)])
    return join(where, y, (heads, splits, tl, group, hd))


def solution(mesh):
    shard = P("kvh", "split", None, None)
    return jax.shard_map(
        per_device,
        mesh=mesh,
        in_specs=(shard,) * 5 + (P("split"), P("split"), P(), P(), P()),
        out_specs=shard,
        check_vma=False,
    )
```

```python
import functools

import jax
import jax.numpy as jnp
from jax import lax
from jax.experimental import pallas as pl
from jax.experimental.pallas import tpu as pltpu
from jax.sharding import PartitionSpec as P

BOTH = ("kvh", "split")
NEG = -1e30
LOG2E = 1.4426950408889634
HUGE = 2.0**100
TINY = 2.0**-120
STEP = 16
TAIL = 4
CHUNK = 64
F32 = jnp.float32
BF16 = jnp.bfloat16

NT = (((1,), (1,)), ((), ()))


def column_bias(lims, page):
    col = lax.broadcasted_iota(jnp.int32, (1, page), 1)
    return jnp.concatenate([jnp.where(col < x, 0.0, NEG) for x in lims], 1)


def pack_kernel(dims, q_hbm, tk_hbm, tv_hbm, o_ref, q_ref, tk_ref, tv_ref, block, sems):
    heads, splits, tl, group, hd = dims
    pairs = ((q_hbm, q_ref), (tk_hbm, tk_ref), (tv_hbm, tv_ref))
    arrivals = [
        pltpu.make_async_copy(src.at[0], dst, sems.at[splits + t])
        for t, (src, dst) in enumerate(pairs)
    ]
    for c in arrivals:
        c.start()
    for c in arrivals:
        c.wait()
    tk = tk_ref[...].astype(F32)
    tv = tv_ref[...].astype(F32)
    for h in range(heads):
        for i in range(tl):
            block[h, i * group : (i + 1) * group, :] = q_ref[
                i, h * group : (h + 1) * group, :
            ]
        both = [t[i, h : h + 1] for t in (tk, tv) for i in range(tl)]
        block[h, tl * group :, :] = jnp.concatenate(both, 0).astype(BF16)
    copies = [
        pltpu.make_async_copy(block, o_ref.at[:, s], sems.at[s]) for s in range(splits)
    ]
    for c in copies:
        c.start()
    for c in copies:
        c.wait()


def pack(queries, tree_keys, tree_values, dims):
    heads, splits, tl, group, hd = dims
    rows = tl * group + 2 * tl
    hbm = pl.BlockSpec(memory_space=pltpu.HBM)
    return pl.pallas_call(
        functools.partial(pack_kernel, dims),
        out_shape=jax.ShapeDtypeStruct((heads, splits, rows, hd), BF16),
        in_specs=[hbm, hbm, hbm],
        out_specs=hbm,
        scratch_shapes=[
            pltpu.VMEM((tl, heads * group, hd), BF16),
            pltpu.VMEM((tl, heads, hd), BF16),
            pltpu.VMEM((tl, heads, hd), BF16),
            pltpu.VMEM((heads, rows, hd), BF16),
            pltpu.SemaphoreType.DMA((splits + 3,)),
        ],
        name="pack",
    )(queries, tree_keys, tree_values)


def prepare_kernel(dims, meta, lists):
    requests, splits, tl, group, pages, page, hd = dims
    i_ctx, i_tl = 2 * pages, 2 * pages + requests
    i_off, i_full, i_edge = pages, pages + requests + 1, pages + 2 * requests + 1
    i_len = pages + 3 * requests + 1
    for r in range(requests):
        lists[i_off + r] = 0
        lists[i_full + r] = 0
        lists[i_edge + r] = 0
        lists[i_len + r] = meta[i_tl + r]
    lists[i_len + requests] = meta[i_tl + requests]

    def tokens(p):
        r = meta[p]
        return r, meta[i_ctx + r] - meta[pages + p] * page

    def count(p, carry):
        r, lim = tokens(p)
        lists[p] = 0
        lists[i_full + r] += jnp.where(lim >= page, 1, 0)
        lists[i_edge + r] += jnp.where((lim > 0) & (lim < page), lim, 0)
        return carry

    lax.fori_loop(0, pages, count, 0)
    total = 0
    for r in range(requests):
        lists[i_off + r] = total
        total += lists[i_full + r] + jnp.where(lists[i_edge + r] > 0, 1, 0)
        lists[i_full + r] = 0
    lists[i_off + requests] = total

    def place(p, carry):
        r, lim = tokens(p)
        n = lists[i_full + r]
        whole = lim >= page

        @pl.when(whole)
        def _():
            lists[lists[i_off + r] + n] = p
            lists[i_full + r] = n + 1

        @pl.when((lim > 0) & (lim < page))
        def _():
            lists[lists[i_off + r + 1] - 1] = p

        return carry

    lax.fori_loop(0, pages, place, 0)


def prepare(meta, dims):
    requests, splits, tl, group, pages, page, hd = dims
    smem = pl.BlockSpec(memory_space=pltpu.SMEM)
    return pl.pallas_call(
        functools.partial(prepare_kernel, dims),
        out_shape=jax.ShapeDtypeStruct((pages + 4 * requests + 2,), jnp.int32),
        in_specs=[smem],
        out_specs=smem,
        compiler_params=pltpu.CompilerParams(vmem_limit_bytes=2**20),
        cost_estimate=pl.CostEstimate(
            flops=0, bytes_accessed=2**24, transcendentals=0
        ),
        name="prepare",
    )(meta)


def attn_kernel(
    dims,
    lists,
    x_ref,
    mask_ref,
    k_hbm,
    v_hbm,
    o_hbm,
    o_ref,
    k_ref,
    v_ref,
    m_s,
    l_s,
    acc,
    top,
    sems,
    out_sems,
):
    requests, splits, tl, group, pages, page, hd = dims
    rows = tl * group
    full_rows = splits * rows
    scale = hd**-0.5 * LOG2E
    i_off, i_full, i_edge = pages, pages + requests + 1, pages + 2 * requests + 1
    i_tl = pages + 3 * requests + 1

    for r in range(requests):

        @pl.loop(lists[i_off + r], lists[i_off + r + 1])
        def _(slot):
            p = lists[slot]
            pltpu.make_async_copy(k_hbm.at[0, p], k_ref.at[slot], sems.at[0, r]).start()
            pltpu.make_async_copy(v_hbm.at[0, p], v_ref.at[slot], sems.at[1, r]).start()

    def arrive(r):
        n = lists[i_off + r + 1] - lists[i_off + r]

        @pl.when(n > 0)
        def _():
            at = pl.ds(0, n)
            for t, (src, dst) in enumerate(((k_hbm, k_ref), (v_hbm, v_ref))):
                pltpu.make_async_copy(src.at[0, at], dst.at[at], sems.at[t, r]).wait()

    me = lists[i_tl + requests]
    per = splits // requests
    tree_request = me // per
    part = me % per
    tree_rows = full_rows // per
    top[...] = jnp.zeros_like(top)

    def queries(r, count):
        blocks = count // rows
        return x_ref[pl.ds(r * splits, blocks), 0:rows, :].reshape(count, hd)

    def tree_page():
        first = pl.multiple_of(part * tree_rows, tree_rows)
        blk = tree_rows // rows
        q = x_ref[pl.ds(tree_request * splits + part * blk, blk), 0:rows, :]
        kv = x_ref[pl.ds(tree_request * splits, splits), rows : rows + 2 * tl, :]
        kv = kv.reshape(splits * 2 * tl, hd)
        wide = splits * 2 * tl
        values = pltpu.roll(kv.astype(F32), wide - tl, 0).astype(BF16)
        drafts = tree_rows // group
        mask = mask_ref[tree_request, pl.ds(part * drafts, drafts), :]
        tree = mask.shape[1]
        src = lax.broadcasted_iota(jnp.int32, (tree, wide), 0)
        dst = lax.broadcasted_iota(jnp.int32, (tree, wide), 1)
        pick = (src // tl == dst // (2 * tl)) & (src % tl == dst % (2 * tl))
        seen = jnp.dot(
            (mask == 1).astype(F32).astype(BF16),
            pick.astype(F32).astype(BF16),
            preferred_element_type=F32,
        )
        bias = jnp.where(seen > 0.5, 0.0, NEG)
        bias = jnp.broadcast_to(bias[:, None, :], (drafts, group, wide))
        s = lax.dot_general(q.reshape(tree_rows, hd), kv, NT, preferred_element_type=F32)
        return first, s + bias.reshape(tree_rows, wide), values

    def whole_block(r, start, nb):
        at = pl.ds(lists[i_off + r] + start, nb)
        return k_ref[at].reshape(nb * page, hd), v_ref[at].reshape(nb * page, hd)

    def pages_of(r):
        return lists[i_off + r + 1] - lists[i_off + r]

    def last_block(r, start, nb):
        n = pages_of(r)
        edge = lists[i_edge + r]
        ids, lims = [], []
        for j in range(nb):
            at = start + j
            ids.append(lists[i_off + r] + jnp.minimum(at, n - 1))
            lims.append(
                jnp.where(at < lists[i_full + r], page, jnp.where(at < n, edge, 0))
            )
        k = jnp.concatenate([k_ref[i] for i in ids], 0)
        v = jnp.concatenate([v_ref[i] for i in ids], 0)
        return k, v, column_bias(lims, page)

    def add(at, where, s, v):
        m = m_s[where, :]
        ps = [
            jnp.exp2(s[:, j : j + page] * scale - m) for j in range(0, s.shape[1], page)
        ]
        l_s[at, :] += functools.reduce(jnp.add, ps)
        p = jnp.concatenate([x.astype(BF16) for x in ps], 1)
        acc[at, :] += jnp.dot(p, v, preferred_element_type=F32)

    def add_online(at, where, s, v):
        old = m_s[where, :]
        new = jnp.maximum(old, jnp.max(s, 1, keepdims=True) * scale)
        m_s[where, :] = new
        fade = jnp.exp2(old - new)
        l_s[at, :] = l_s[at, :] * fade
        acc[at, :] = acc[at, :] * fade
        add(at, where, s, v)

    def finish(r, count):
        blocks = count // rows
        total = jnp.sum(l_s[0:count, :], 1, keepdims=True)
        total = jnp.broadcast_to(total, (count, hd))
        o = (acc[0:count, :] / jnp.maximum(total, TINY)).astype(BF16)
        o_ref[pl.ds(r * splits, blocks), 0:rows, :] = o.reshape(blocks, rows, hd)
        lane = lax.broadcasted_iota(jnp.int32, (1, 1, hd), 2)
        span = hd // tl

        def by_lane(x):
            x = x.reshape(blocks, tl, group, hd)
            out = x[:, tl - 1]
            for i in range(tl - 2, -1, -1):
                out = jnp.where(lane < (i + 1) * span, x[:, i], out)
            return out

        sums = by_lane(total)
        shift = by_lane(m_s[pl.ds(r * full_rows, count), :])
        both = jnp.where(sums > 0.0, shift + jnp.log2(jnp.maximum(sums, TINY)), NEG)
        high = both.astype(BF16).astype(F32)
        mid = (both - high).astype(BF16).astype(F32)
        low = both - high - mid
        inner = lane % span
        stat = jnp.where(inner == 0, high, jnp.where(inner == 1, mid, low))
        o_ref[pl.ds(r * splits, blocks), rows : rows + group, :] = stat.astype(BF16)
        return total

    @pl.loop(0, requests)
    def _(r):
        for b in range(splits):
            for i in range(tl):
                block = r * splits + b
                q = x_ref[block, i * group : (i + 1) * group, :].astype(F32)
                key = x_ref[block, rows + i : rows + i + 1, :].astype(F32)
                s = jnp.sum(q * key, 1, keepdims=True) * scale
                at = pl.multiple_of(block * rows + i * group, group)
                m_s[pl.ds(at, group), :] = jnp.broadcast_to(s, (group, hd))

    def send(r):
        at = pl.ds(r * splits, splits)
        return pltpu.make_async_copy(o_ref.at[at], o_hbm.at[at], out_sems.at[r])

    def rows_of(r, first, count):
        return pl.ds(pl.multiple_of(r * full_rows + first, 8), count)

    def request(r, count):
        at = slice(0, count)
        where = rows_of(r, 0, count)
        l_s[...] = jnp.zeros_like(l_s)
        acc[...] = jnp.zeros_like(acc)

        @pl.when(r == tree_request)
        def _():
            first, s, v = tree_page()
            add(pl.ds(first, tree_rows), rows_of(r, first, tree_rows), s, v)

        q = queries(r, count)

        def take(start, nb):
            k, v = whole_block(r, start, nb)
            add(at, where, lax.dot_general(q, k, NT, preferred_element_type=F32), v)

        whole = lists[i_full + r] // STEP

        @pl.loop(0, whole)
        def _(b):
            take(b * STEP, STEP)

        start = whole * STEP
        quarters = (pages_of(r) - start + TAIL - 1) // TAIL
        for c in range(1, STEP // TAIL + 1):

            @pl.when(quarters == c)
            def _(c=c):
                k, v, bias = last_block(r, start + (c - 1) * TAIL, TAIL)
                if c > 1:
                    k0, v0 = whole_block(r, start, (c - 1) * TAIL)
                    k, v = jnp.concatenate([k0, k], 0), jnp.concatenate([v0, v], 0)
                s = lax.dot_general(q, k, NT, preferred_element_type=F32)
                edge = (c - 1) * TAIL * page
                last = s[:, edge:] + bias
                s = jnp.concatenate([s[:, :edge], last], 1) if c > 1 else last
                add(at, where, s, v)

        total = finish(r, count)
        high = functools.reduce(
            jnp.maximum, [total[j : j + 8] for j in range(0, count, 8)]
        )
        top[...] = jnp.maximum(top[...], high)

    def request_online(r):
        at = slice(0, full_rows)
        where = rows_of(r, 0, full_rows)
        m_s[where, :] = jnp.full((full_rows, hd), NEG, F32)
        l_s[...] = jnp.zeros_like(l_s)
        acc[...] = jnp.zeros_like(acc)

        @pl.when(r == tree_request)
        def _():
            first, s, v = tree_page()
            add_online(pl.ds(first, tree_rows), rows_of(r, first, tree_rows), s, v)

        q = queries(r, full_rows)

        @pl.loop(0, (pages_of(r) + 1) // 2)
        def _(b):
            k, v, bias = last_block(r, b * 2, 2)
            s = lax.dot_general(q, k, NT, preferred_element_type=F32)
            add_online(at, where, s + bias, v)

        finish(r, full_rows)

    @pl.loop(0, requests)
    def _(r):
        arrive(r)
        chunks = (lists[i_tl + r] * group + CHUNK - 1) // CHUNK
        for c in range(2, full_rows // CHUNK + 1):

            @pl.when((chunks == c) | ((c == 2) & (chunks < 2)))
            def _():
                request(r, c * CHUNK)

        send(r).start()

    for r in range(requests):
        send(r).wait()

    @pl.when(jnp.logical_not(jnp.max(top[...]) < HUGE))
    def _():
        @pl.loop(0, requests)
        def _(r):
            request_online(r)
            send(r).start()
            send(r).wait()


def attend(lists, x, mask, key_cache, value_cache, dims):
    requests, splits, tl, group, pages, page, hd = dims
    full_rows = splits * tl * group
    smem = pl.BlockSpec(memory_space=pltpu.SMEM)
    vmem = pl.BlockSpec(memory_space=pltpu.VMEM)
    hbm = pl.BlockSpec(memory_space=pltpu.HBM)
    return pl.pallas_call(
        functools.partial(attn_kernel, dims),
        out_shape=jax.ShapeDtypeStruct(x.shape, BF16),
        in_specs=[smem, vmem, vmem, hbm, hbm],
        out_specs=hbm,
        scratch_shapes=[
            pltpu.VMEM(x.shape, BF16),
            pltpu.VMEM((pages, page, hd), BF16),
            pltpu.VMEM((pages, page, hd), BF16),
            pltpu.VMEM((requests * full_rows, hd), F32),
            pltpu.VMEM((full_rows, hd), F32),
            pltpu.VMEM((full_rows, hd), F32),
            pltpu.VMEM((8, hd), F32),
            pltpu.SemaphoreType.DMA((2, requests)),
            pltpu.SemaphoreType.DMA((requests,)),
        ],
        compiler_params=pltpu.CompilerParams(vmem_limit_bytes=48 * 2**20),
        name="attend",
    )(lists, x, mask, key_cache, value_cache)


def join_kernel(dims, where_ref, y_ref, o_ref):
    heads, splits, tl, group, hd = dims
    rows = tl * group
    span = hd // tl
    src = lax.broadcasted_iota(jnp.int32, (hd, tl * hd), 0)
    dst = lax.broadcasted_iota(jnp.int32, (hd, tl * hd), 1)
    pick = (src // span == dst // hd) & (src % span < 3)
    pick = pick.astype(F32).astype(BF16)
    first = where_ref[0]
    length = where_ref[1]
    for h in range(heads):
        stat = y_ref[h * splits : (h + 1) * splits, rows : rows + group, :]
        lse = jnp.dot(
            stat.reshape(splits * group, hd), pick, preferred_element_type=F32
        )
        for i in range(tl):
            one = lse[:, i * hd : (i + 1) * hd].reshape(splits, group, hd)
            high = jnp.max(one, 0, keepdims=True)
            w = jnp.exp2(one - high)
            o = y_ref[
                h * splits : (h + 1) * splits, i * group : (i + 1) * group, :
            ].astype(F32)
            res = jnp.sum(w * o, 0) / jnp.sum(w, 0)
            res = jnp.where(first + i < length, res, 0.0)
            o_ref[0, i, h * group : (h + 1) * group, :] = res.astype(BF16)


def join(where, y, dims):
    heads, splits, tl, group, hd = dims
    return pl.pallas_call(
        functools.partial(join_kernel, dims),
        out_shape=jax.ShapeDtypeStruct((1, tl, heads * group, hd), BF16),
        in_specs=[
            pl.BlockSpec(memory_space=pltpu.SMEM),
            pl.BlockSpec(memory_space=pltpu.VMEM),
        ],
        out_specs=pl.BlockSpec(memory_space=pltpu.VMEM),
        compiler_params=pltpu.CompilerParams(vmem_limit_bytes=16 * 2**20),
        name="join",
    )(where, y)


def per_device(
    queries,
    tree_keys,
    tree_values,
    key_cache,
    value_cache,
    page_request,
    page_index,
    ctx_len,
    tree_len,
    tree_mask,
):
    heads = lax.axis_size("kvh")
    splits = lax.axis_size("split")
    unused, tl, hq, hd = queries.shape
    group = hq // heads
    requests = ctx_len.shape[0]
    unused, pages, page, unused = key_cache.shape
    me = lax.axis_index("split").astype(jnp.int32)

    x = pack(queries, tree_keys, tree_values, (heads, splits, tl, group, hd))
    x = x.reshape((heads * splits,) + x.shape[2:])
    x = lax.all_to_all(x, BOTH, 0, 0, tiled=True)

    meta = jnp.concatenate([page_request, page_index, ctx_len, tree_len, me[None]])
    dims = (requests, splits, tl, group, pages, page, hd)
    lists = prepare(meta, dims)
    y = attend(lists, x, tree_mask, key_cache, value_cache, dims)

    y = lax.all_to_all(y, BOTH, 0, 0, tiled=True)
    own = lax.axis_index("kvh")
    where = jnp.stack([me * tl, jnp.take(tree_len, own)])
    return join(where, y, (heads, splits, tl, group, hd))


def solution(mesh):
    shard = P("kvh", "split", None, None)
    return jax.shard_map(
        per_device,
        mesh=mesh,
        in_specs=(shard,) * 5 + (P("split"), P("split"), P(), P(), P()),
        out_specs=shard,
        check_vma=False,
    )
```
